32 devices in a mesh: rows: 16 (over z, y, core), img: 2 (over x).
Axes of the slice: x: 2, y: 2, z: 4, core: 2. Of those that a mesh axis runs over, the one named last changes fastest.
Arguments:
- image_in: float32 [16, 256, 88, 128], P('img', 'rows'), may hold values from -30 to 30, as said below
- gain_one: float32 [128], replicated, may hold values from 0.1 to 1.9
- shift_one: float32 [128], replicated, may hold values from -3 to 3
- kernel_one: float32 [3, 3, 128, 128], replicated, may hold values from -0.1875 to 0.1875
- bias_one: float32 [128], replicated, may hold values from -3 to 3
- gain_two: float32 [128], replicated, may hold values from 0.1 to 1.9
- shift_two: float32 [128], replicated, may hold values from -3 to 3
- kernel_two: float32 [3, 3, 128, 128], replicated, may hold values from -0.1875 to 0.1875
- bias_two: float32 [128], replicated, may hold values from -3 to 3
- out_grad: float32 [16, 2, 16, 8, 88, 128], P('rows', 'img'), may hold values from -30 to 30, as said below
Outputs:
- mixed: float32 [16, 2, 16, 8, 88, 128], P('rows', 'img')
- input_grad: float32 [16, 256, 88, 128], P('img', 'rows')
- gain_one_grad: float32 [128], replicated
- shift_one_grad: float32 [128], replicated
- kernel_one_grad: float32 [3, 3, 128, 128], replicated
- bias_one_grad: float32 [128], replicated
- gain_two_grad: float32 [128], replicated
- shift_two_grad: float32 [128], replicated
- kernel_two_grad: float32 [3, 3, 128, 128], replicated
- bias_two_grad: float32 [128], replicated
The draws below stay inside these ranges and needn't reach their ends.
Inputs may be any that keep to these rules, and one draw needn't show every extreme that they name: `image_in`: feature map of order one with per-channel offsets and scales. `out_grad`: gradient of order one.
All inputs are finite; a program needn't handle non-finite values.
Results may differ from the reference program's by a relative error of at most 0.0003.
Values sent between devices are 32-bit elements; how exact they have to be, the bound alone decides.
No kernel may reach another device: no remote copies, remote signals or barrier semaphores. Data moves between devices by JAX's collectives and lax.ppermute only.
A program may use at most 256 MiB of HBM per device.

```python
import jax
import jax.numpy as jnp
from jax import lax

CHANNELS = 128
GROUPS = 32
HEIGHT = 256
WIDTH = 88
IMAGES = 16
SLAB = 8
N_ROWS = 16
N_IMG = 2


def row_rise(number, start, ratio):
    position = jnp.arange(number, dtype=jnp.float32) / (number - 1.0)
    return start * jnp.power(ratio, position)


def draw_image_in(key, part):
    key = jax.random.fold_in(key, 11)
    keys = jax.random.split(key, 3)
    layout = (IMAGES, HEIGHT, WIDTH, CHANNELS)
    base = jnp.clip(jax.random.normal(keys[0], layout, jnp.float32), -5.0, 5.0)
    rising = row_rise(HEIGHT, 0.5, 3.0)
    offset = 0.5 * jnp.clip(jax.random.normal(keys[1], (IMAGES, 1, 1, CHANNELS), jnp.float32), -3.0, 3.0)
    channel_scale = jnp.exp(jax.random.uniform(keys[2], (1, 1, 1, CHANNELS), jnp.float32, -1.1, 1.1))
    return (offset + base) * channel_scale * rising[None, :, None, None]


def draw_out_grad(key, part):
    key = jax.random.fold_in(key, 23)
    keys = jax.random.split(key, 3)
    layout = (IMAGES, N_IMG, N_ROWS, SLAB, WIDTH, CHANNELS)
    base = jnp.clip(jax.random.normal(keys[0], layout, jnp.float32), -5.0, 5.0)
    rising = row_rise(N_ROWS, 0.5, 3.0)
    channel_scale = jnp.exp(jax.random.uniform(keys[1], (1, 1, 1, 1, 1, CHANNELS), jnp.float32, -0.7, 0.7))
    offset = jnp.clip(jax.random.normal(keys[2], (IMAGES, 1, 1, 1, 1, CHANNELS), jnp.float32), -3.0, 3.0)
    return (offset + base) * channel_scale * rising[None, None, :, None, None, None]


def normal_values(own_key, shape, scale, reach, kind=jnp.bfloat16):
    drawn = jax.random.normal(own_key, shape, jnp.float32) * scale
    return jnp.minimum(jnp.maximum(drawn, -reach), reach).astype(kind)


def setup_inputs(seed: int = 0) -> dict:
    key_of = jax.random.split(jax.random.key(seed), 11)
    image_in = draw_image_in(jax.random.fold_in(key_of[10], 71), 0)
    gain_one = jnp.clip(1.0 + 0.18 * jax.random.normal(key_of[1], (CHANNELS,), jnp.float32), 0.1, 1.9)
    shift_one = normal_values(key_of[2], (CHANNELS,), 0.5, 3.0, jnp.float32)
    kernel_one = normal_values(key_of[3], (3, 3, CHANNELS, CHANNELS), (9 * CHANNELS) ** -0.5, 0.1875, jnp.float32)
    bias_one = normal_values(key_of[4], (CHANNELS,), 0.5, 3.0, jnp.float32)
    gain_two = jnp.clip(1.0 + 0.18 * jax.random.normal(key_of[5], (CHANNELS,), jnp.float32), 0.1, 1.9)
    shift_two = normal_values(key_of[6], (CHANNELS,), 0.5, 3.0, jnp.float32)
    kernel_two = normal_values(key_of[7], (3, 3, CHANNELS, CHANNELS), (9 * CHANNELS) ** -0.5, 0.1875, jnp.float32)
    bias_two = normal_values(key_of[8], (CHANNELS,), 0.5, 3.0, jnp.float32)
    out_grad = draw_out_grad(jax.random.fold_in(key_of[10], 71), 0)
    return dict(image_in=image_in, gain_one=gain_one, shift_one=shift_one, kernel_one=kernel_one, bias_one=bias_one, gain_two=gain_two, shift_two=shift_two, kernel_two=kernel_two, bias_two=bias_two, out_grad=out_grad)


EPSILON = 1e-06

@jax.custom_vjp
def low(v):
    return lax.optimization_barrier(v.astype(jnp.bfloat16)).astype(jnp.float32)

@jax.custom_vjp
def low_back(v):
    return v

def low_keep(v):
    return (low(v), None)

def low_pass(kept, grad):
    return (grad,)

def back_keep(v):
    return (v, None)

def back_low(kept, grad):
    return (low(grad),)
low.defvjp(low_keep, low_pass)
low_back.defvjp(back_keep, back_low)

def group_norm(tensor, gain, shift):
    grouped = tensor.reshape(HEIGHT, WIDTH, GROUPS, CHANNELS // GROUPS)
    means = lax.optimization_barrier(jnp.mean(grouped, axis=(0, 1, 3), keepdims=True))
    centered = grouped - means
    spread = lax.optimization_barrier(jnp.mean(centered * centered, axis=(0, 1, 3), keepdims=True))
    normed = (centered * lax.rsqrt(spread + EPSILON)).reshape(HEIGHT, WIDTH, CHANNELS)
    return normed * gain + shift

def convolve(tensor, kernel, bias):
    output = lax.conv_general_dilated(tensor[None], kernel, (1, 1), ((1, 1), (1, 1)), dimension_numbers=('NHWC', 'HWIO', 'NHWC'), precision=lax.Precision.HIGHEST)
    return output[0] + bias

def block(picture, gain_one, shift_one, kernel_one, bias_one, gain_two, shift_two, kernel_two, bias_two):
    middle = convolve(jax.nn.silu(group_norm(picture, gain_one, shift_one)), kernel_one, bias_one)
    return picture + convolve(jax.nn.silu(group_norm(middle, gain_two, shift_two)), kernel_two, bias_two)

def reference(image_in, gain_one, shift_one, kernel_one, bias_one, gain_two, shift_two, kernel_two, bias_two, out_grad):
    spatial_grad = out_grad.transpose(0, 2, 1, 3, 4, 5).reshape(IMAGES, HEIGHT, WIDTH, CHANNELS)
    params = (gain_one, shift_one, kernel_one, bias_one, gain_two, shift_two, kernel_two, bias_two)

    def step(carry, item):
        picture, cotangent = item
        result, pullback = jax.vjp(block, picture, *params)
        grads = pullback(cotangent)
        updated = tuple((held + fresh for held, fresh in zip(carry, grads[1:])))
        return (updated, (result, grads[0]))
    initial = tuple((jnp.zeros_like(param) for param in params))
    sums, outputs = lax.scan(step, initial, (image_in, spatial_grad))
    results, input_grad = outputs
    mixed = results.reshape(IMAGES, N_ROWS, N_IMG, SLAB, WIDTH, CHANNELS).transpose(0, 2, 1, 3, 4, 5)
    return (mixed, input_grad, sums[0], sums[1], sums[2], sums[3], sums[4], sums[5], sums[6], sums[7])
```

```python
import functools

import jax
import jax.numpy as jnp
from jax import lax
from jax.experimental import pallas as pl
from jax.experimental.pallas import tpu as pltpu
from jax.sharding import PartitionSpec as P

GROUPS = 32
EPSILON = 1e-06
BF16 = jnp.bfloat16
F32 = jnp.float32
MARGIN = 8


def kernel_params():
    return pltpu.CompilerParams(vmem_limit_bytes=48 * 2**20)


def cost(flops, nbytes):
    return pl.CostEstimate(flops=int(flops), bytes_accessed=int(nbytes), transcendentals=0)


def split(x):
    high = x.astype(BF16)
    return high, (x - high.astype(F32)).astype(BF16)


def widen(x):
    return jnp.concatenate([x, jnp.zeros((x.shape[0], MARGIN, x.shape[2]), F32)], axis=1)


def put_split(s_ref, row, x):
    channels = x.shape[2]
    high, low = split(widen(x))
    s_ref[row : row + x.shape[0], :, 0:channels] = high
    s_ref[row : row + x.shape[0], :, channels:] = low


def conv_rows(s_ref, w_ref, row, rows):
    wide, channels = s_ref.shape[1], s_ref.shape[2] // 2
    m = rows * wide
    parts = [s_ref[row + a : row + a + rows].reshape(m, 2 * channels) for a in range(3)]
    parts += [s_ref[row + a : row + a + rows, :, 0:channels].reshape(m, channels) for a in range(3)]
    y = jnp.dot(jnp.concatenate(parts, axis=1), w_ref[...], preferred_element_type=F32)
    out = y[:, channels : 2 * channels]
    out = out + pltpu.roll(y[:, :channels], 1, 0) + pltpu.roll(y[:, 2 * channels :], m - 1, 0)
    return out.reshape(rows, wide, channels)[:, : wide - MARGIN]


def row_blocks(total, size):
    return [(r, min(size, total - r)) for r in range(0, total, size)]


def silu(v):
    return v * jax.nn.sigmoid(v)


def silu_slope(v):
    s = jax.nn.sigmoid(v)
    return s * (1.0 + v * (1.0 - s))


def total(x):
    return jnp.sum(x.reshape(-1, x.shape[-1]), axis=0, keepdims=True)


def put_stats(out_ref, i, x):
    count = x.shape[0] * x.shape[1]
    added = total(x)
    mean = added * (1.0 / count)
    off = x - mean[None]
    out_ref[0, pl.ds(i, 1), :] = added
    out_ref[1, pl.ds(i, 1), :] = total(off * off)


def stats_kernel(x_ref, out_ref):
    put_stats(out_ref, pl.program_id(0), x_ref[0])


def conv_one_kernel(edge_ref, x_ref, top_ref, bot_ref, n_ref, w_ref, b_ref, mid_ref, act_ref, stat_ref, s_ref):
    i = pl.program_id(0)
    rows = x_ref.shape[1]
    mean, scale, shift = n_ref[0, pl.ds(i, 1)], n_ref[1, pl.ds(i, 1)], n_ref[2, pl.ds(i, 1)]
    act = lambda v: silu((v - mean[None]) * scale[None] + shift[None])
    put_split(s_ref, 0, act(top_ref[0]) * edge_ref[0])
    put_split(s_ref, 2, act(x_ref[0]))
    put_split(s_ref, 2 + rows, act(bot_ref[0]) * edge_ref[1])
    act_ref[0] = s_ref[1 : rows + 3]
    for r, size in row_blocks(rows + 2, 6):
        mid_ref[0, r : r + size] = conv_rows(s_ref, w_ref, r, size) + b_ref[...][None]
    put_stats(stat_ref, i, mid_ref[0, 1 : rows + 1])


def conv_two_kernel(edge_ref, mid_ref, x_ref, n_ref, w_ref, b_ref, out_ref, act_ref):
    i = pl.program_id(0)
    rows = x_ref.shape[1]
    mean, scale, shift = n_ref[0, pl.ds(i, 1)], n_ref[1, pl.ds(i, 1)], n_ref[2, pl.ds(i, 1)]
    act = lambda v: silu((v - mean[None]) * scale[None] + shift[None])
    s_ref = act_ref.at[0]
    put_split(s_ref, 0, act(mid_ref[0, 0:1]) * edge_ref[0])
    put_split(s_ref, 1, act(mid_ref[0, 1 : rows + 1]))
    put_split(s_ref, 1 + rows, act(mid_ref[0, rows + 1 :]) * edge_ref[1])
    for r, size in row_blocks(rows, 8):
        out_ref[0, r : r + size] = conv_rows(s_ref, w_ref, r, size) + b_ref[...][None] + x_ref[0, r : r + size]


def back_two_kernel(g_ref, top_ref, bot_ref, mid_ref, n_ref, w_ref, out_ref, sum_ref, s_ref):
    i = pl.program_id(0)
    rows = g_ref.shape[1]
    mean, scale, shift, rstd = (n_ref[k, pl.ds(i, 1)][None] for k in range(4))
    put_split(s_ref, 0, top_ref[0])
    put_split(s_ref, 2, g_ref[0])
    put_split(s_ref, 2 + rows, bot_ref[0])
    sum_ref[2, pl.ds(i, 1), :] = total(g_ref[0])
    for r, size in row_blocks(rows + 2, 6):
        off = mid_ref[0, r : r + size] - mean
        out_ref[0, r : r + size] = conv_rows(s_ref, w_ref, r, size) * silu_slope(off * scale + shift)
    own = out_ref[0, 1 : rows + 1]
    sum_ref[0, pl.ds(i, 1), :] = total(own)
    sum_ref[1, pl.ds(i, 1), :] = total(own * ((mid_ref[0, 1 : rows + 1] - mean) * rstd))


def add_kernel_grad(act_ref, g, out_ref, g_scr):
    wide, channels = act_ref.shape[2], act_ref.shape[3] // 2
    rows = act_ref.shape[1] - 2
    m = rows * wide
    flat = widen(g).reshape(m, channels)
    for c, turned in enumerate((pltpu.roll(flat, m - 1, 0), flat, pltpu.roll(flat, 1, 0))):
        high, low = split(turned)
        g_scr[:, c * channels : (c + 1) * channels] = high
        g_scr[:, (c + 3) * channels : (c + 4) * channels] = low
    over_pixels = (((0,), (0,)), ((), ()))
    n = 3 * channels
    for a in range(3):
        high = act_ref[0, a : a + rows, :, 0:channels].reshape(m, channels)
        low = act_ref[0, a : a + rows, :, channels:].reshape(m, channels)
        p = lax.dot_general(high, g_scr[...], over_pixels, preferred_element_type=F32)
        q = lax.dot_general(low, g_scr[:, :n], over_pixels, preferred_element_type=F32)
        out_ref[a] += p[:, :n] + p[:, n:] + q


def grad_two_kernel(act_ref, g_ref, out_ref, g_scr):
    @pl.when(pl.program_id(0) == 0)
    def _():
        out_ref[...] = jnp.zeros_like(out_ref)

    add_kernel_grad(act_ref, g_ref[0], out_ref, g_scr)


def grad_one_kernel(edge_ref, act_ref, pre_ref, mid_ref, n_ref, out_ref, sum_ref, gm_ref, g_scr):
    i = pl.program_id(0)

    @pl.when(i == 0)
    def _():
        out_ref[...] = jnp.zeros_like(out_ref)

    rows = act_ref.shape[1] - 2
    mean, rstd, gain, first, second = (n_ref[k, pl.ds(i, 1)][None] for k in range(5))

    def back(r, size):
        normed = (mid_ref[0, r : r + size] - mean) * rstd
        return rstd * (pre_ref[0, r : r + size] * gain - first - normed * second)

    own = back(1, rows)
    s_ref = gm_ref.at[0]
    put_split(s_ref, 0, back(0, 1) * edge_ref[0])
    put_split(s_ref, 1, own)
    put_split(s_ref, 1 + rows, back(rows + 1, 1) * edge_ref[1])
    sum_ref[0, pl.ds(i, 1), :] = total(own)
    add_kernel_grad(act_ref, own, out_ref, g_scr)


def back_one_kernel(gm_ref, x_ref, n_ref, w_ref, out_ref, sum_ref):
    i = pl.program_id(0)
    rows = x_ref.shape[1]
    mean, scale, shift, rstd = (n_ref[k, pl.ds(i, 1)][None] for k in range(4))
    s_ref = gm_ref.at[0]
    for r, size in row_blocks(rows, 8):
        off = x_ref[0, r : r + size] - mean
        out_ref[0, r : r + size] = conv_rows(s_ref, w_ref, r, size) * silu_slope(off * scale + shift)
    own = out_ref[0]
    sum_ref[0, pl.ds(i, 1), :] = total(own)
    sum_ref[1, pl.ds(i, 1), :] = total(own * ((x_ref[0] - mean) * rstd))


def final_kernel(g_ref, pre_ref, x_ref, n_ref, out_ref):
    i = pl.program_id(0)
    mean, rstd, gain, first, second = (n_ref[k, pl.ds(i, 1)][None] for k in range(5))
    normed = (x_ref[0] - mean) * rstd
    out_ref[0] = g_ref[0] + rstd * (pre_ref[0] * gain - first - normed * second)


def same_group(channels):
    width = channels // GROUPS
    row = lax.broadcasted_iota(jnp.int32, (channels, channels), 0) // width
    col = lax.broadcasted_iota(jnp.int32, (channels, channels), 1) // width
    return (row == col).astype(F32)


def over_group(x):
    return jnp.dot(x, same_group(x.shape[-1]), precision=lax.Precision.HIGHEST, preferred_element_type=F32)


def norm_kernel(all_ref, gain_ref, shift_ref, out_ref, *, local):
    devices, _, _, channels = all_ref.shape
    count = devices * local * (channels // GROUPS)
    added = all_ref[:, 0]
    mean = over_group(jnp.sum(added, axis=0)) * (1.0 / count)
    off = added * (1.0 / local) - mean[None]
    spread = over_group(jnp.sum(all_ref[:, 1] + off * off * float(local), axis=0)) * (1.0 / count)
    rstd = lax.rsqrt(spread + EPSILON)
    out_ref[0] = mean
    out_ref[1] = rstd * gain_ref[...]
    out_ref[2] = jnp.broadcast_to(shift_ref[...], mean.shape)
    out_ref[3] = rstd


def back_norm_kernel(all_ref, n_ref, gain_ref, out_ref, *, local):
    devices, _, _, channels = all_ref.shape
    count = devices * local * (channels // GROUPS)
    out_ref[0] = n_ref[0]
    out_ref[1] = n_ref[3]
    out_ref[2] = jnp.broadcast_to(gain_ref[...], n_ref[0].shape)
    for k in range(2):
        out_ref[3 + k] = over_group(jnp.sum(all_ref[:, k], axis=0) * gain_ref[...]) * (1.0 / count)


def per_image(shape):
    rest = len(shape) - 1
    return pl.BlockSpec((1,) + tuple(shape[1:]), lambda i: (i,) + (0,) * rest)


def whole(shape):
    return pl.BlockSpec(tuple(shape), lambda i: (0,) * len(shape))


SCALARS = pl.BlockSpec(memory_space=pltpu.SMEM)


def call(kernel, images, ins, outs, scratch=(), flops=0):
    nbytes = sum(x.size * x.dtype.itemsize for x, _ in ins)
    shapes = [jax.ShapeDtypeStruct(shape, dtype) for shape, dtype, _ in outs]
    nbytes += sum(s.size * s.dtype.itemsize for s in shapes)
    return pl.pallas_call(
        kernel,
        grid=(images,),
        in_specs=[spec for _, spec in ins],
        out_specs=[spec for _, _, spec in outs],
        out_shape=shapes,
        scratch_shapes=list(scratch),
        compiler_params=kernel_params(),
        cost_estimate=cost(flops, nbytes),
    )(*[x for x, _ in ins])


def img(x):
    return (x, per_image(x.shape))


def all_(x):
    return (x, whole(x.shape))


def small_call(kernel, ins, shape):
    return pl.pallas_call(kernel, out_shape=jax.ShapeDtypeStruct(shape, F32))(*ins)


def prepare(kernel):
    high = lax.reduce_precision(kernel, 8, 7)
    low = kernel - high
    lay = lambda k: jnp.transpose(k, (0, 2, 1, 3)).reshape(3, k.shape[2], -1)
    h, l = lay(high), lay(low)
    return jnp.concatenate([h[0], h[0], h[1], h[1], h[2], h[2], l[0], l[1], l[2]], axis=0).astype(BF16)


def turned(kernel):
    return jnp.transpose(kernel[::-1, ::-1], (0, 1, 3, 2))


def gather_small(x):
    count = lax.axis_size("rows")
    return lax.all_to_all(jnp.broadcast_to(x[None], (count,) + x.shape), "rows", 0, 0)


def halo(x, width):
    count = lax.axis_size("rows")
    forward = [(i, i + 1) for i in range(count - 1)]
    backward = [(b, a) for a, b in forward]
    top = lax.ppermute(x[:, x.shape[1] - width :], "rows", forward)
    bottom = lax.ppermute(x[:, :width], "rows", backward)
    return top, bottom


def to_batch(result):
    images, row_count, col_count, channels = result.shape
    row_devs = lax.axis_size("rows")
    img_devs = lax.axis_size("img")
    slab = row_count // img_devs
    batch_dev = images * img_devs // row_devs
    section_one = lax.all_to_all(result, "img", split_axis=1, concat_axis=0, tiled=True)
    section_two = lax.all_to_all(section_one, "rows", split_axis=0, concat_axis=1, tiled=True)
    return section_two.reshape(batch_dev, 1, row_devs, slab, col_count, channels)


def to_space(out_grad):
    batch_dev, single, row_devs, slab, col_count, channels = out_grad.shape
    flat = out_grad.reshape(batch_dev, row_devs * slab, col_count, channels)
    section_one = lax.all_to_all(flat, "rows", split_axis=1, concat_axis=0, tiled=True)
    return lax.all_to_all(section_one, "img", split_axis=0, concat_axis=1, tiled=True)


def shards(
    image_in, gain_one, shift_one, kernel_one, bias_one, gain_two, shift_two, kernel_two, bias_two, out_grad
):
    n, rows, cols, ch = image_in.shape
    local = rows * cols
    ext = rows + 2
    wide = cols + MARGIN
    place = lax.axis_index("rows")
    edge = jnp.stack([place > 0, place < lax.axis_size("rows") - 1]).astype(F32)
    edges = (edge, SCALARS)
    row_vec = lambda v: v[None, :]
    conv_flops = 2 * 9 * ch * ch * cols * 3 * n
    pair_shape = (2, n, ch)
    pair = (pair_shape, F32, whole(pair_shape))
    maps = lambda r: ((n, r, cols, ch), F32, per_image((n, r, cols, ch)))
    splits = lambda r: ((n, r, wide, 2 * ch), BF16, per_image((n, r, wide, 2 * ch)))
    taps = ((3, ch, 3 * ch), F32, whole((3, ch, 3 * ch)))
    norm = functools.partial(norm_kernel, local=local)
    back_norm = functools.partial(back_norm_kernel, local=local)

    w_one, w_two = prepare(kernel_one), prepare(kernel_two)
    w_one_back, w_two_back = prepare(turned(kernel_one)), prepare(turned(kernel_two))

    (stat_one,) = call(stats_kernel, n, [img(image_in)], [pair])
    n_one = small_call(norm, (gather_small(stat_one), row_vec(gain_one), row_vec(shift_one)), (4, n, ch))
    top, bottom = halo(image_in, 2)
    middle, act_one, stat_two = call(
        conv_one_kernel,
        n,
        [edges, img(image_in), img(top), img(bottom), all_(n_one), all_(w_one), all_(row_vec(bias_one))],
        [maps(ext), splits(ext), pair],
        [pltpu.VMEM((rows + 4, wide, 2 * ch), BF16)],
        conv_flops * ext,
    )
    n_two = small_call(norm, (gather_small(stat_two), row_vec(gain_two), row_vec(shift_two)), (4, n, ch))
    result, act_two = call(
        conv_two_kernel,
        n,
        [edges, img(middle), img(image_in), all_(n_two), all_(w_two), all_(row_vec(bias_two))],
        [maps(rows), splits(ext)],
        (),
        conv_flops * rows,
    )
    mixed = to_batch(result)

    grad_result = to_space(out_grad)
    g_top, g_bottom = halo(grad_result, 2)
    sums_shape = (3, n, ch)
    pre_two, sum_two = call(
        back_two_kernel,
        n,
        [img(grad_result), img(g_top), img(g_bottom), img(middle), all_(n_two), all_(w_two_back)],
        [maps(ext), (sums_shape, F32, whole(sums_shape))],
        [pltpu.VMEM((rows + 4, wide, 2 * ch), BF16)],
        conv_flops * ext,
    )
    b_two = small_call(back_norm, (gather_small(sum_two[:2]), n_two, row_vec(gain_two)), (5, n, ch))
    g_scr = pltpu.VMEM((rows * wide, 6 * ch), BF16)
    (taps_two,) = call(grad_two_kernel, n, [img(act_two), img(grad_result)], [taps], [g_scr], conv_flops * rows)
    one_shape = (1, n, ch)
    taps_one, sum_mid, grad_mid = call(
        grad_one_kernel,
        n,
        [edges, img(act_one), img(pre_two), img(middle), all_(b_two)],
        [taps, (one_shape, F32, whole(one_shape)), splits(ext)],
        [g_scr],
        conv_flops * rows,
    )
    pre_one, sum_one = call(
        back_one_kernel,
        n,
        [img(grad_mid), img(image_in), all_(n_one), all_(w_one_back)],
        [maps(rows), pair],
        (),
        conv_flops * rows,
    )
    b_one = small_call(back_norm, (gather_small(sum_one), n_one, row_vec(gain_one)), (5, n, ch))
    (input_grad,) = call(final_kernel, n, [img(grad_result), img(pre_one), img(image_in), all_(b_one)], [maps(rows)])

    vectors = jnp.sum(jnp.concatenate([sum_one, sum_mid, sum_two], axis=0), axis=1)
    everywhere = ("rows", "img")
    untap = lambda t: jnp.transpose(t.reshape(3, ch, 3, ch), (0, 2, 1, 3))
    grad_kernel_two = untap(lax.psum(taps_two, everywhere))
    grad_kernel_one = untap(lax.psum(taps_one, everywhere))
    vectors = lax.psum(vectors, everywhere)
    return (
        mixed,
        input_grad,
        vectors[1],
        vectors[0],
        grad_kernel_one,
        vectors[2],
        vectors[4],
        vectors[3],
        grad_kernel_two,
        vectors[5],
    )


def solution(mesh):
    spread = P("img", "rows", None, None)
    banded = P("rows", "img", None, None, None, None)
    return jax.shard_map(
        shards,
        mesh=mesh,
        in_specs=(spread,) + (P(),) * 8 + (banded,),
        out_specs=(banded, spread) + (P(),) * 8,
        check_vma=False,
    )
```

```python
import functools

import jax
import jax.numpy as jnp
from jax import lax
from jax.experimental import pallas as pl
from jax.experimental.pallas import tpu as pltpu
from jax.sharding import PartitionSpec as P

GROUPS = 32
EPSILON = 1e-06
BF16 = jnp.bfloat16
F32 = jnp.float32
MARGIN = 8


def kernel_params():
    return pltpu.CompilerParams(vmem_limit_bytes=48 * 2**20)


def cost(flops, nbytes):
    return pl.CostEstimate(flops=int(flops) // 64, bytes_accessed=int(nbytes) // 64, transcendentals=0)


def split(x):
    high = x.astype(BF16)
    return high, (x - high.astype(F32)).astype(BF16)


def widen(x):
    return jnp.concatenate([x, jnp.zeros((x.shape[0], MARGIN, x.shape[2]), F32)], axis=1)


def put_split(s_ref, row, x):
    channels = x.shape[2]
    high, low = split(widen(x))
    s_ref[row : row + x.shape[0], :, 0:channels] = high
    s_ref[row : row + x.shape[0], :, channels:] = low


def conv_rows(s_ref, w_ref, row, rows):
    wide, channels = s_ref.shape[1], s_ref.shape[2] // 2
    m = rows * wide
    parts = [s_ref[row + a : row + a + rows].reshape(m, 2 * channels) for a in range(3)]
    parts += [s_ref[row + a : row + a + rows, :, 0:channels].reshape(m, channels) for a in range(3)]
    y = jnp.dot(jnp.concatenate(parts, axis=1), w_ref[...], preferred_element_type=F32)
    out = y[:, channels : 2 * channels]
    out = out + pltpu.roll(y[:, :channels], 1, 0) + pltpu.roll(y[:, 2 * channels :], m - 1, 0)
    return out.reshape(rows, wide, channels)[:, : wide - MARGIN]


def row_blocks(total, size):
    return [(r, min(size, total - r)) for r in range(0, total, size)]


def silu(v):
    return v * jax.nn.sigmoid(v)


def silu_slope(v):
    s = jax.nn.sigmoid(v)
    return s * (1.0 + v * (1.0 - s))


def total(x):
    return jnp.sum(x.reshape(-1, x.shape[-1]), axis=0, keepdims=True)


def put_stats(out_ref, i, x):
    count = x.shape[0] * x.shape[1]
    added = total(x)
    mean = added * (1.0 / count)
    off = x - mean[None]
    out_ref[0, pl.ds(i, 1), :] = added
    out_ref[1, pl.ds(i, 1), :] = total(off * off)


def stats_kernel(x_ref, out_ref):
    put_stats(out_ref, pl.program_id(0), x_ref[0])


def conv_one_kernel(edge_ref, x_ref, top_ref, bot_ref, n_ref, w_ref, b_ref, mid_ref, act_ref, stat_ref, s_ref):
    i = pl.program_id(0)
    rows = x_ref.shape[1]
    mean, scale, shift = n_ref[0, pl.ds(i, 1)], n_ref[1, pl.ds(i, 1)], n_ref[2, pl.ds(i, 1)]
    act = lambda v: silu((v - mean[None]) * scale[None] + shift[None])
    put_split(s_ref, 0, act(top_ref[0]) * edge_ref[0])
    put_split(s_ref, 2, act(x_ref[0]))
    put_split(s_ref, 2 + rows, act(bot_ref[0]) * edge_ref[1])
    act_ref[0] = s_ref[1 : rows + 3]
    for r, size in row_blocks(rows + 2, 6):
        mid_ref[0, r : r + size] = conv_rows(s_ref, w_ref, r, size) + b_ref[...][None]
    put_stats(stat_ref, i, mid_ref[0, 1 : rows + 1])


def conv_two_kernel(edge_ref, mid_ref, x_ref, n_ref, w_ref, b_ref, out_ref, act_ref):
    i = pl.program_id(0)
    rows = x_ref.shape[1]
    slab = out_ref.shape[2]
    mean, scale, shift = n_ref[0, pl.ds(i, 1)], n_ref[1, pl.ds(i, 1)], n_ref[2, pl.ds(i, 1)]
    act = lambda v: silu((v - mean[None]) * scale[None] + shift[None])
    s_ref = act_ref.at[0]
    put_split(s_ref, 0, act(mid_ref[0, 0:1]) * edge_ref[0])
    put_split(s_ref, 1, act(mid_ref[0, 1 : rows + 1]))
    put_split(s_ref, 1 + rows, act(mid_ref[0, rows + 1 :]) * edge_ref[1])
    for r, size in row_blocks(rows, slab):
        out_ref[r // slab, 0] = conv_rows(s_ref, w_ref, r, size) + b_ref[...][None] + x_ref[0, r : r + size]


def back_two_kernel(band_ref, top_ref, bot_ref, mid_ref, n_ref, w_ref, *refs, offsets):
    pieces, (g_ref, out_ref, sum_ref, s_ref) = refs[:-4], refs[-4:]
    i = pl.program_id(0)
    count = len(offsets)
    rows = g_ref.shape[1]
    mean, scale, shift, rstd = (n_ref[k, pl.ds(i, 1)][None] for k in range(4))
    for d in range(len(pieces) // count):
        for s, at in enumerate(offsets):
            piece = pieces[d * count + s]
            _, slab, cols, _ = piece.shape
            g_ref[0, pl.ds(band_ref[d] * slab, slab), at : at + cols, :] = piece[0]
    put_split(s_ref, 0, top_ref[0])
    put_split(s_ref, 2, g_ref[0])
    put_split(s_ref, 2 + rows, bot_ref[0])
    for r, size in row_blocks(rows + 2, 6):
        off = mid_ref[0, r : r + size] - mean
        out_ref[0, r : r + size] = conv_rows(s_ref, w_ref, r, size) * silu_slope(off * scale + shift)
    own = out_ref[0, 1 : rows + 1]
    sum_ref[0, pl.ds(i, 1), :] = total(own)
    sum_ref[1, pl.ds(i, 1), :] = total(own * ((mid_ref[0, 1 : rows + 1] - mean) * rstd))


def add_kernel_grad(act_ref, g, out_ref, g_scr):
    wide, channels = act_ref.shape[2], act_ref.shape[3] // 2
    rows = act_ref.shape[1] - 2
    m = rows * wide
    flat = widen(g).reshape(m, channels)
    for c, turned in enumerate((pltpu.roll(flat, m - 1, 0), flat, pltpu.roll(flat, 1, 0))):
        high, low = split(turned)
        g_scr[:, c * channels : (c + 1) * channels] = high
        g_scr[:, (c + 3) * channels : (c + 4) * channels] = low
    over_pixels = (((0,), (0,)), ((), ()))
    n = 3 * channels
    for a in range(3):
        high = act_ref[0, a : a + rows, :, 0:channels].reshape(m, channels)
        low = act_ref[0, a : a + rows, :, channels:].reshape(m, channels)
        p = lax.dot_general(high, g_scr[...], over_pixels, preferred_element_type=F32)
        q = lax.dot_general(low, g_scr[:, :n], over_pixels, preferred_element_type=F32)
        both = p[:, :n] + p[:, n:] + q
        for c in range(3):
            out_ref[3 * a + c] += both[:, c * channels : (c + 1) * channels]


def grad_two_kernel(act_ref, g_ref, out_ref, sum_ref, g_scr):
    i = pl.program_id(0)

    @pl.when(i == 0)
    def _():
        out_ref[...] = jnp.zeros_like(out_ref)

    g = g_ref[0]
    sum_ref[0, pl.ds(i, 1), :] = total(g)
    add_kernel_grad(act_ref, g, out_ref, g_scr)


def grad_one_kernel(edge_ref, act_ref, pre_ref, mid_ref, n_ref, out_ref, sum_ref, gm_ref, g_scr):
    i = pl.program_id(0)

    @pl.when(i == 0)
    def _():
        out_ref[...] = jnp.zeros_like(out_ref)

    rows = act_ref.shape[1] - 2
    mean, rstd, gain, first, second = (n_ref[k, pl.ds(i, 1)][None] for k in range(5))

    def back(r, size):
        normed = (mid_ref[0, r : r + size] - mean) * rstd
        return rstd * (pre_ref[0, r : r + size] * gain - first - normed * second)

    own = back(1, rows)
    s_ref = gm_ref.at[0]
    put_split(s_ref, 0, back(0, 1) * edge_ref[0])
    put_split(s_ref, 1, own)
    put_split(s_ref, 1 + rows, back(rows + 1, 1) * edge_ref[1])
    sum_ref[0, pl.ds(i, 1), :] = total(own)
    add_kernel_grad(act_ref, own, out_ref, g_scr)


def back_one_kernel(gm_ref, x_ref, n_ref, w_ref, out_ref, sum_ref):
    i = pl.program_id(0)
    rows = x_ref.shape[1]
    mean, scale, shift, rstd = (n_ref[k, pl.ds(i, 1)][None] for k in range(4))
    s_ref = gm_ref.at[0]
    for r, size in row_blocks(rows, 8):
        off = x_ref[0, r : r + size] - mean
        out_ref[0, r : r + size] = conv_rows(s_ref, w_ref, r, size) * silu_slope(off * scale + shift)
    own = out_ref[0]
    sum_ref[0, pl.ds(i, 1), :] = total(own)
    sum_ref[1, pl.ds(i, 1), :] = total(own * ((x_ref[0] - mean) * rstd))


def final_kernel(g_ref, pre_ref, x_ref, n_ref, out_ref):
    i = pl.program_id(0)
    mean, rstd, gain, first, second = (n_ref[k, pl.ds(i, 1)][None] for k in range(5))
    normed = (x_ref[0] - mean) * rstd
    out_ref[0] = g_ref[0] + rstd * (pre_ref[0] * gain - first - normed * second)


def same_group(channels):
    width = channels // GROUPS
    row = lax.broadcasted_iota(jnp.int32, (channels, channels), 0) // width
    col = lax.broadcasted_iota(jnp.int32, (channels, channels), 1) // width
    return (row == col).astype(F32)


def over_group(x):
    return jnp.dot(x, same_group(x.shape[-1]), precision=lax.Precision.HIGHEST, preferred_element_type=F32)


def norm_kernel(all_ref, gain_ref, shift_ref, out_ref, *, local):
    devices, _, _, channels = all_ref.shape
    count = devices * local * (channels // GROUPS)
    added = all_ref[:, 0]
    mean = over_group(jnp.sum(added, axis=0)) * (1.0 / count)
    off = added * (1.0 / local) - mean[None]
    spread = over_group(jnp.sum(all_ref[:, 1] + off * off * float(local), axis=0)) * (1.0 / count)
    rstd = lax.rsqrt(spread + EPSILON)
    out_ref[0] = mean
    out_ref[1] = rstd * gain_ref[...]
    out_ref[2] = jnp.broadcast_to(shift_ref[...], mean.shape)
    out_ref[3] = rstd


def back_norm_kernel(all_ref, n_ref, gain_ref, out_ref, *, local):
    devices, _, _, channels = all_ref.shape
    count = devices * local * (channels // GROUPS)
    out_ref[0] = n_ref[0]
    out_ref[1] = n_ref[3]
    out_ref[2] = jnp.broadcast_to(gain_ref[...], n_ref[0].shape)
    for k in range(2):
        out_ref[3 + k] = over_group(jnp.sum(all_ref[:, k], axis=0) * gain_ref[...]) * (1.0 / count)


def per_image(shape):
    rest = len(shape) - 1
    return pl.BlockSpec((1,) + tuple(shape[1:]), lambda i: (i,) + (0,) * rest)


def whole(shape):
    return pl.BlockSpec(tuple(shape), lambda i: (0,) * len(shape))


SCALARS = pl.BlockSpec(memory_space=pltpu.SMEM)


def call(kernel, images, ins, outs, scratch=(), flops=0):
    nbytes = sum(x.size * x.dtype.itemsize for x, _ in ins)
    shapes = [jax.ShapeDtypeStruct(shape, dtype) for shape, dtype, _ in outs]
    nbytes += sum(s.size * s.dtype.itemsize for s in shapes)
    return pl.pallas_call(
        kernel,
        grid=(images,),
        in_specs=[spec for _, spec in ins],
        out_specs=[spec for _, _, spec in outs],
        out_shape=shapes,
        scratch_shapes=list(scratch),
        compiler_params=kernel_params(),
        cost_estimate=cost(flops, nbytes),
    )(*[x for x, _ in ins])


def img(x):
    return (x, per_image(x.shape))


def all_(x):
    return (x, whole(x.shape))


def small_call(kernel, ins, shape):
    return pl.pallas_call(kernel, out_shape=jax.ShapeDtypeStruct(shape, F32))(*ins)


def weights_kernel(*refs):
    count = len(refs) // 3
    for k in range(count):
        k_ref = refs[k]
        ch = k_ref.shape[2]
        for turned in (False, True):
            out_ref = refs[count + 2 * k + turned]
            for a in range(3):
                for c in range(3):
                    w = k_ref[2 - a, 2 - c].T if turned else k_ref[a, c]
                    high, low = split(w)
                    at = slice(c * ch, (c + 1) * ch)
                    out_ref[2 * a * ch : (2 * a + 1) * ch, at] = high
                    out_ref[(2 * a + 1) * ch : (2 * a + 2) * ch, at] = high
                    out_ref[(6 + a) * ch : (7 + a) * ch, at] = low


def prepare(*kernels):
    ch = kernels[0].shape[2]
    shape = jax.ShapeDtypeStruct((9 * ch, 3 * ch), BF16)
    return pl.pallas_call(weights_kernel, out_shape=[shape] * (2 * len(kernels)), compiler_params=kernel_params())(*kernels)


def after(x, *others):
    return lax.optimization_barrier((x,) + others)[0]


def partner(x, axis, bit):
    return lax.ppermute(x, axis, [(k, k ^ bit) for k in range(lax.axis_size(axis))])


def bits(axis):
    return [1 << k for k in range(lax.axis_size(axis).bit_length() - 1)]


def far_bits():
    low, high = bits("rows")[-2:]
    return low, high, low + high


def gather_sums(x, join):
    for bit in bits("rows")[:-2]:
        x = join(x, partner(x, "rows", bit), bit)
    return jnp.stack([x] + [partner(x, "rows", bit) for bit in far_bits()])


def shift_rows(top_source, bottom_source):
    count = lax.axis_size("rows")
    forward = [(i, i + 1) for i in range(count - 1)]
    backward = [(b, a) for a, b in forward]
    return lax.ppermute(top_source, "rows", forward), lax.ppermute(bottom_source, "rows", backward)


def shift_bands(band):
    row_devs, count = lax.axis_size("rows"), lax.axis_size("img")
    me = lax.axis_index("img")
    edge = jnp.where(me == 0, band[:, :2], band[:, band.shape[1] - 2 :])
    edge = edge.reshape((count, -1) + edge.shape[1:])
    got = []
    for s in range(count):
        down, up = (count - 1 + s) % count, s
        block = lax.dynamic_index_in_dim(edge, jnp.where(me == 0, up, down), 0, keepdims=False)
        pairs = [(r * count + count - 1, (r + 1) * count + down) for r in range(row_devs - 1)]
        pairs += [(r * count, (r - 1) * count + up) for r in range(1, row_devs)]
        got.append(lax.ppermute(block, ("rows", "img"), pairs))
    got = jnp.stack(got)
    pick = lambda k: lax.dynamic_index_in_dim(got, k, 0, keepdims=False)
    return pick(lax.rem(me + 1, count)), pick(me)


def rotate_img(blocks):
    count = lax.axis_size("img")
    me = lax.axis_index("img")
    pick = lambda k: lax.dynamic_index_in_dim(blocks, lax.rem(k, count), 0, keepdims=False)
    came = [pick(me)]
    for d in range(1, count):
        came.append(lax.ppermute(pick(me + d), "img", [(k, (k + d) % count) for k in range(count)]))
    return came


def img_sources():
    count = lax.axis_size("img")
    me = lax.axis_index("img")
    return [lax.rem(me - d + count, count) for d in range(count)]


def slices(cols, shares):
    units, cuts, seen = cols // 8, [0], 0
    for share in shares[:-1]:
        seen += share
        cuts.append(8 * round(units * seen / sum(shares)))
    cuts.append(cols)
    return [(a, b) for a, b in zip(cuts, cuts[1:]) if b > a]


def swap_rows(x):
    return lax.all_to_all(x, "rows", 0, 0)


def trade(x, axis, bit):
    half = x.shape[0] // 2
    mine = lax.rem(lax.axis_index(axis) // bit, 2)
    keep = lax.dynamic_slice_in_dim(x, mine * half, half, 0)
    give = lax.dynamic_slice_in_dim(x, (1 - mine) * half, half, 0)
    return keep + partner(give, axis, bit)


def untrade(x, axis, bit):
    mine = lax.rem(lax.axis_index(axis) // bit, 2)
    other = partner(x, axis, bit)
    return jnp.where(mine == 0, jnp.concatenate([x, other]), jnp.concatenate([other, x]))


def far_place():
    return lax.axis_index("rows") // far_bits()[0]


def far_trade(x):
    quarter = x.shape[0] // 4
    part = lambda k: lax.dynamic_slice_in_dim(x, k * quarter, quarter, 0)
    place = far_place()
    kept = part(place)
    for d, bit in enumerate(far_bits()):
        kept = kept + partner(part(place ^ (d + 1)), "rows", bit)
    return kept


def far_untrade(x):
    parts = jnp.stack([x] + [partner(x, "rows", bit) for bit in far_bits()])
    place = far_place()
    return jnp.concatenate([lax.dynamic_index_in_dim(parts, place ^ k, 0, keepdims=False) for k in range(4)])


def shards(
    image_in, gain_one, shift_one, kernel_one, bias_one, gain_two, shift_two, kernel_two, bias_two, out_grad
):
    n, rows, cols, ch = image_in.shape
    local = rows * cols
    ext = rows + 2
    wide = cols + MARGIN
    place = lax.axis_index("rows")
    edge = jnp.stack([place > 0, place < lax.axis_size("rows") - 1]).astype(F32)
    edges = (edge, SCALARS)
    row_vec = lambda v: v[None, :]
    conv_flops = 2 * 9 * ch * ch * cols * 3 * n
    pair_shape = (2, n, ch)
    pair = (pair_shape, F32, whole(pair_shape))
    maps = lambda r: ((n, r, cols, ch), F32, per_image((n, r, cols, ch)))
    splits = lambda r: ((n, r, wide, 2 * ch), BF16, per_image((n, r, wide, 2 * ch)))
    taps = ((9, ch, ch), F32, whole((9, ch, ch)))
    row_devs, img_devs = lax.axis_size("rows"), lax.axis_size("img")
    slab = rows // img_devs
    in_cuts = slices(cols, (2, 5, 4))
    out_cuts = slices(cols, (3, 5, 3))
    me = lax.axis_index("img")
    norm = functools.partial(norm_kernel, local=local * row_devs // 4)
    back_norm = functools.partial(back_norm_kernel, local=local * row_devs // 4)
    back_norm_last = functools.partial(back_norm_kernel, local=local * row_devs)
    one_shape = (1, n, ch)
    one = (one_shape, F32, whole(one_shape))
    g_scr = pltpu.VMEM((rows * wide, 6 * ch), BF16)

    def join_spread(x, y, bit):
        off = x[0] - y[0]
        return jnp.stack([x[0] + y[0], x[1] + y[1] + off * off * (0.5 / (bit * local))])

    def join_add(x, y, bit):
        return x + y

    grad_in = out_grad.reshape(out_grad.shape[2:])
    landed, came = [], []

    def bring(k, *others):
        a, b = in_cuts[k]
        landed.append(swap_rows(after(grad_in[:, :, a:b], *others)))

    def settle(k, *others):
        a, b = in_cuts[k]
        came.append(rotate_img(after(landed[k], *others).reshape(img_devs, n, slab, b - a, ch)))

    w_one, w_one_back, w_two, w_two_back = prepare(kernel_one, kernel_two)

    top, bottom = shift_rows(image_in[:, rows - 2 :], image_in[:, :2])
    (stat_one,) = call(stats_kernel, n, [img(image_in)], [pair])
    bring(0, stat_one)
    far_one = after(gather_sums(stat_one, join_spread), landed[0], top, bottom)
    n_one = small_call(norm, (far_one, row_vec(gain_one), row_vec(shift_one)), (4, n, ch))
    bring(1, far_one)
    settle(0, far_one)
    middle, act_one, stat_two = call(
        conv_one_kernel,
        n,
        [edges, img(image_in), img(top), img(bottom), all_(n_one), all_(w_one), all_(row_vec(bias_one))],
        [maps(ext), splits(ext), pair],
        [pltpu.VMEM((rows + 4, wide, 2 * ch), BF16)],
        conv_flops * ext,
    )
    far_two = after(gather_sums(after(stat_two, *came[0]), join_spread), landed[1])
    n_two = small_call(norm, (far_two, row_vec(gain_two), row_vec(shift_two)), (4, n, ch))
    bring(2, far_two)
    settle(1, far_two)
    banded_shape = (img_devs, n, slab, cols, ch)
    banded = (banded_shape, F32, pl.BlockSpec((img_devs, 1, slab, cols, ch), lambda i: (0, i, 0, 0, 0)))
    result, act_two = call(
        conv_two_kernel,
        n,
        [edges, img(middle), img(image_in), all_(n_two), all_(w_two), all_(row_vec(bias_two))],
        [banded, splits(ext)],
        (),
        conv_flops * rows,
    )

    def turn(a, b, *others):
        bands = jnp.stack(rotate_img(after(result[..., a:b, :], *others)))
        pick = lambda j: lax.dynamic_index_in_dim(bands, lax.rem(me - j + img_devs, img_devs), 0, keepdims=False)
        return jnp.stack([pick(j) for j in range(img_devs)]).reshape(img_devs * n, slab, b - a, ch)

    mixed_parts = []

    def send(k, *others):
        mixed_parts.append(swap_rows(after(blocks[k], *others)))

    early = out_cuts[0][1]
    first_turned = turn(0, early, *came[1])
    settle(2, first_turned)
    last_turned = turn(early, cols, *came[2])
    blocks = [
        first_turned[:, :, a:b] if b <= early else last_turned[:, :, a - early : b - early] for a, b in out_cuts
    ]

    halves = [shift_bands(jnp.concatenate(landed[:-1], axis=2)), shift_bands(landed[-1])]
    g_top, g_bottom = (jnp.concatenate([half[k] for half in halves], axis=2) for k in range(2))
    send(0, landed[2], blocks[0], g_top, g_bottom)
    pieces = [[part[d] for part in came] for d in range(img_devs)]
    offsets = tuple(a for a, _ in in_cuts)
    band = jnp.stack(img_sources()).astype(jnp.int32)
    grad_result, pre_two, sum_two = call(
        functools.partial(back_two_kernel, offsets=offsets),
        n,
        [(band, SCALARS), img(g_top), img(g_bottom), img(middle), all_(n_two), all_(w_two_back)]
        + [img(p) for line in pieces for p in line],
        [maps(rows), maps(ext), pair],
        [pltpu.VMEM((rows + 4, wide, 2 * ch), BF16)],
        conv_flops * ext,
    )
    far_back = after(gather_sums(sum_two, join_add), mixed_parts[0], last_turned)
    b_two = small_call(back_norm, (far_back, n_two, row_vec(gain_two)), (5, n, ch))
    send(1, far_back)
    taps_two, sum_grad = call(
        grad_two_kernel,
        n,
        [img(act_two), img(after(grad_result, far_back))],
        [taps, one],
        [g_scr],
        conv_flops * rows,
    )
    taps_one, sum_mid, grad_mid = call(
        grad_one_kernel,
        n,
        [edges, img(act_one), img(pre_two), img(middle), all_(b_two)],
        [taps, one, splits(ext)],
        [g_scr],
        conv_flops * rows,
    )
    size = 9 * ch
    flat = jnp.concatenate([taps_one.reshape(size, ch), taps_two.reshape(size, ch)])
    steps = [("rows", bits("rows")[0])] + [("img", k) for k in bits("img")] + [("rows", k) for k in bits("rows")[1:-2]]
    for axis, bit in steps:
        flat = trade(flat, axis, bit)
    grad_mid = after(grad_mid, flat)
    pre_one, sum_one = call(
        back_one_kernel,
        n,
        [img(grad_mid), img(image_in), all_(n_one), all_(w_one_back)],
        [maps(rows), pair],
        (),
        conv_flops * rows,
    )
    sums = jnp.concatenate([sum_one, sum_mid, sum_grad], axis=0)
    for bit in bits("rows")[:-2]:
        sums = sums + partner(sums, "rows", bit)
    both = after(jnp.concatenate([sums.reshape(-1, ch), flat]), mixed_parts[1])
    both = both + sum(partner(both, "rows", bit) for bit in far_bits())
    far_last, flat = both[: sums.size // ch].reshape((1,) + sums.shape), both[sums.size // ch :]
    b_one = small_call(back_norm_last, (far_last, n_one, row_vec(gain_one)), (5, n, ch))
    send(2, far_last, flat)
    (input_grad,) = call(final_kernel, n, [img(grad_result), img(pre_one), img(image_in), all_(b_one)], [maps(rows)])
    flat = after(flat, input_grad)
    for axis, bit in reversed(steps):
        flat = untrade(flat, axis, bit)
    vectors = jnp.concatenate([jnp.sum(far_last, axis=(0, 2)), jnp.sum(far_back, axis=(0, 2))])
    for bit in bits("img"):
        vectors = vectors + partner(vectors, "img", bit)
    mixed_parts[-1] = after(mixed_parts[-1], input_grad, flat, vectors)
    grad_kernel_one, grad_kernel_two = (k.reshape(3, 3, ch, ch) for k in (flat[:size], flat[size:]))
    mixed = jnp.concatenate(mixed_parts, axis=2)[None, None]
    return (
        mixed,
        input_grad,
        vectors[1],
        vectors[0],
        grad_kernel_one,
        vectors[2],
        vectors[5],
        vectors[4],
        grad_kernel_two,
        vectors[3],
    )


def solution(mesh):
    spread = P("img", "rows", None, None)
    banded = P("rows", "img", None, None, None, None)
    return jax.shard_map(
        shards,
        mesh=mesh,
        in_specs=(spread,) + (P(),) * 8 + (banded,),
        out_specs=(banded, spread) + (P(),) * 8,
        check_vma=False,
    )
```

```python
import functools

import jax
import jax.numpy as jnp
from jax import lax
from jax.experimental import pallas as pl
from jax.experimental.pallas import tpu as pltpu
from jax.sharding import PartitionSpec as P

GROUPS = 32
EPSILON = 1e-06
BF16 = jnp.bfloat16
F32 = jnp.float32
MARGIN = 8


def kernel_params():
    return pltpu.CompilerParams(vmem_limit_bytes=48 * 2**20)


def cost(flops, nbytes):
    return pl.CostEstimate(flops=int(flops) // 64, bytes_accessed=int(nbytes) // 64, transcendentals=0)


def split(x):
    high = x.astype(BF16)
    return high, (x - high.astype(F32)).astype(BF16)


def widen(x):
    return jnp.concatenate([x, jnp.zeros((x.shape[0], MARGIN, x.shape[2]), F32)], axis=1)


def put_split(s_ref, row, x):
    channels = x.shape[2]
    high, low = split(widen(x))
    s_ref[row : row + x.shape[0], :, 0:channels] = high
    s_ref[row : row + x.shape[0], :, channels:] = low


def conv_rows(s_ref, w_ref, low_ref, row, rows):
    wide, channels = s_ref.shape[1], s_ref.shape[2] // 2
    m, n = rows * wide, 3 * channels
    high = [s_ref[row + a : row + a + rows, :, 0:channels].reshape(m, channels) for a in range(3)]
    low = [s_ref[row + a : row + a + rows, :, channels:].reshape(m, channels) for a in range(3)]
    y = jnp.dot(jnp.concatenate(high + low[2:], axis=1), w_ref[...], preferred_element_type=F32)
    y = y[:, :n] + y[:, n:]
    y = y + jnp.dot(jnp.concatenate(low[:2], axis=1), low_ref[...], preferred_element_type=F32)
    out = y[:, channels : 2 * channels]
    out = out + pltpu.roll(y[:, :channels], 1, 0) + pltpu.roll(y[:, 2 * channels :], m - 1, 0)
    return out.reshape(rows, wide, channels)[:, : wide - MARGIN]


def row_blocks(total, size):
    return [(r, min(size, total - r)) for r in range(0, total, size)]


def silu(v):
    return v * jax.nn.sigmoid(v)


def silu_slope(v):
    s = jax.nn.sigmoid(v)
    return s * (1.0 + v * (1.0 - s))


def total(x):
    return jnp.sum(x.reshape(-1, x.shape[-1]), axis=0, keepdims=True)


def put_stats(out_ref, i, x):
    count = x.shape[0] * x.shape[1]
    added = total(x)
    mean = added * (1.0 / count)
    off = x - mean[None]
    out_ref[0, pl.ds(i, 1), :] = added
    out_ref[1, pl.ds(i, 1), :] = total(off * off)


def stats_kernel(x_ref, out_ref):
    put_stats(out_ref, pl.program_id(0), x_ref[0])


def conv_one_kernel(edge_ref, x_ref, top_ref, bot_ref, n_ref, w_ref, low_ref, b_ref, mid_ref, act_ref, stat_ref, s_ref):
    i = pl.program_id(0)
    rows = x_ref.shape[1]
    mean, scale, shift = n_ref[0, pl.ds(i, 1)], n_ref[1, pl.ds(i, 1)], n_ref[2, pl.ds(i, 1)]
    act = lambda v: silu((v - mean[None]) * scale[None] + shift[None])
    put_split(s_ref, 0, act(top_ref[0]) * edge_ref[0])
    put_split(s_ref, 2, act(x_ref[0]))
    put_split(s_ref, 2 + rows, act(bot_ref[0]) * edge_ref[1])
    act_ref[0] = s_ref[1 : rows + 3]
    for r, size in row_blocks(rows + 2, 6):
        mid_ref[0, r : r + size] = conv_rows(s_ref, w_ref, low_ref, r, size) + b_ref[...][None]
    put_stats(stat_ref, i, mid_ref[0, 1 : rows + 1])


def conv_two_kernel(edge_ref, mid_ref, x_ref, n_ref, w_ref, low_ref, b_ref, out_ref, act_ref):
    i = pl.program_id(0)
    rows = x_ref.shape[1]
    slab = out_ref.shape[2]
    mean, scale, shift = n_ref[0, pl.ds(i, 1)], n_ref[1, pl.ds(i, 1)], n_ref[2, pl.ds(i, 1)]
    act = lambda v: silu((v - mean[None]) * scale[None] + shift[None])
    s_ref = act_ref.at[0]
    put_split(s_ref, 0, act(mid_ref[0, 0:1]) * edge_ref[0])
    put_split(s_ref, 1, act(mid_ref[0, 1 : rows + 1]))
    put_split(s_ref, 1 + rows, act(mid_ref[0, rows + 1 :]) * edge_ref[1])
    for r, size in row_blocks(rows, slab):
        out_ref[r // slab, 0] = conv_rows(s_ref, w_ref, low_ref, r, size) + b_ref[...][None] + x_ref[0, r : r + size]


def back_two_kernel(band_ref, top_ref, bot_ref, mid_ref, n_ref, w_ref, low_ref, *refs, offsets):
    pieces, (g_ref, out_ref, sum_ref, s_ref) = refs[:-4], refs[-4:]
    i = pl.program_id(0)
    count = len(offsets)
    rows = g_ref.shape[1]
    mean, scale, shift, rstd = (n_ref[k, pl.ds(i, 1)][None] for k in range(4))
    for d in range(len(pieces) // count):
        for s, at in enumerate(offsets):
            piece = pieces[d * count + s]
            _, slab, cols, _ = piece.shape
            g_ref[0, pl.ds(band_ref[d] * slab, slab), at : at + cols, :] = piece[0]
    put_split(s_ref, 0, top_ref[0])
    put_split(s_ref, 1, g_ref[0])
    put_split(s_ref, 1 + rows, bot_ref[0])
    sums = [jnp.zeros((1, g_ref.shape[3]), F32)] * 2
    for r, size in row_blocks(rows, 8):
        off = mid_ref[0, r + 1 : r + 1 + size] - mean
        grad = conv_rows(s_ref, w_ref, low_ref, r, size) * silu_slope(off * scale + shift)
        out_ref[0, r : r + size] = grad
        sums = [sums[0] + total(grad), sums[1] + total(grad * (off * rstd))]
    sum_ref[0, pl.ds(i, 1), :] = sums[0]
    sum_ref[1, pl.ds(i, 1), :] = sums[1]


def taps_kernel(before_ref, act_ref, *refs, offsets, start):
    band_ref, pieces, (out_ref, sum_ref, g_ref, g_scr) = refs[0], refs[1:-4], refs[-4:]
    channels = g_ref.shape[2]
    rows, width, _ = g_ref.shape
    m = rows * width
    i = pl.program_id(0)

    @pl.when(i == 0)
    def _():
        out_ref[...] = before_ref[...]
        g_ref[...] = jnp.zeros_like(g_ref)

    count = len(offsets)
    for k in range(len(pieces) // count):
        for s, at in enumerate(offsets):
            piece = pieces[k * count + s]
            _, slab, cols, _ = piece.shape
            g_ref[pl.ds(band_ref[k] * slab, slab), at : at + cols, :] = piece[0]
    flat = g_ref[...].reshape(m, channels)
    sum_ref[0, pl.ds(i, 1), :] = total(flat)
    column = lax.broadcasted_iota(jnp.int32, (rows, width, channels), 1).reshape(m, channels)
    right = jnp.where(column < width - 1, pltpu.roll(flat, m - 1, 0), 0.0)
    for c, shifted in enumerate((right, flat, pltpu.roll(flat, 1, 0))):
        high, low = split(shifted)
        g_scr[:, c * channels : (c + 1) * channels] = high
        g_scr[:, (c + 3) * channels : (c + 4) * channels] = low
    over_pixels = (((0,), (0,)), ((), ()))
    n = 3 * channels
    for a in range(3):
        high = act_ref[0, a : a + rows, start : start + width, 0:channels].reshape(m, channels)
        low = act_ref[0, a : a + rows, start : start + width, channels:].reshape(m, channels)
        p = lax.dot_general(high, g_scr[...], over_pixels, preferred_element_type=F32)
        q = lax.dot_general(low, g_scr[:, :n], over_pixels, preferred_element_type=F32)
        both = p[:, :n] + p[:, n:] + q
        for c in range(3):
            out_ref[3 * a + c] += both[:, c * channels : (c + 1) * channels]


def back_one_kernel(edge_ref, pre_ref, top_ref, bot_ref, mid_ref, b_ref, g_ref, x_ref, n_ref, w_ref, low_ref, gm_ref, out_ref, sum_ref, s_ref):
    i = pl.program_id(0)
    rows = x_ref.shape[1]
    mid_mean, mid_rstd, gain, first, second = (b_ref[k, pl.ds(i, 1)][None] for k in range(5))
    mean, scale, shift, rstd = (n_ref[k, pl.ds(i, 1)][None] for k in range(4))

    def back(pre, mid):
        normed = (mid - mid_mean) * mid_rstd
        return mid_rstd * (pre * gain - first - normed * second)

    own = back(pre_ref[0], mid_ref[0, 1 : rows + 1])
    gm_ref[0] = own
    put_split(s_ref, 0, back(top_ref[0], mid_ref[0, 0:1]) * edge_ref[0])
    put_split(s_ref, 1, own)
    put_split(s_ref, 1 + rows, back(bot_ref[0], mid_ref[0, rows + 1 :]) * edge_ref[1])
    sum_ref[2, pl.ds(i, 1), :] = total(own)
    sums = [jnp.zeros((1, x_ref.shape[3]), F32)] * 2
    for r, size in row_blocks(rows, 8):
        off = x_ref[0, r : r + size] - mean
        grad = conv_rows(s_ref, w_ref, low_ref, r, size) * silu_slope(off * scale + shift)
        out_ref[0, r : r + size] = g_ref[0, r : r + size] + scale * grad
        sums = [sums[0] + total(grad), sums[1] + total(grad * (off * rstd))]
    sum_ref[0, pl.ds(i, 1), :] = sums[0]
    sum_ref[1, pl.ds(i, 1), :] = sums[1]


def final_kernel(u_ref, x_ref, n_ref, out_ref):
    i = pl.program_id(0)
    mean, rstd, _, first, second = (n_ref[k, pl.ds(i, 1)][None] for k in range(5))
    out_ref[0] = u_ref[0] - rstd * (first + (x_ref[0] - mean) * rstd * second)


def same_group(channels):
    width = channels // GROUPS
    row = lax.broadcasted_iota(jnp.int32, (channels, channels), 0) // width
    col = lax.broadcasted_iota(jnp.int32, (channels, channels), 1) // width
    return (row == col).astype(F32)


def over_group(x):
    return jnp.dot(x, same_group(x.shape[-1]), precision=lax.Precision.HIGHEST, preferred_element_type=F32)


def norm_kernel(all_ref, gain_ref, shift_ref, out_ref, *, local):
    devices, _, _, channels = all_ref.shape
    count = devices * local * (channels // GROUPS)
    added = all_ref[:, 0]
    mean = over_group(jnp.sum(added, axis=0)) * (1.0 / count)
    off = added * (1.0 / local) - mean[None]
    spread = over_group(jnp.sum(all_ref[:, 1] + off * off * float(local), axis=0)) * (1.0 / count)
    rstd = lax.rsqrt(spread + EPSILON)
    out_ref[0] = mean
    out_ref[1] = rstd * gain_ref[...]
    out_ref[2] = jnp.broadcast_to(shift_ref[...], mean.shape)
    out_ref[3] = rstd


def back_norm_kernel(all_ref, n_ref, gain_ref, out_ref, *, local):
    devices, _, _, channels = all_ref.shape
    count = devices * local * (channels // GROUPS)
    out_ref[0] = n_ref[0]
    out_ref[1] = n_ref[3]
    out_ref[2] = jnp.broadcast_to(gain_ref[...], n_ref[0].shape)
    for k in range(2):
        out_ref[3 + k] = over_group(jnp.sum(all_ref[:, k], axis=0) * gain_ref[...]) * (1.0 / count)


def per_image(shape):
    rest = len(shape) - 1
    return pl.BlockSpec((1,) + tuple(shape[1:]), lambda i: (i,) + (0,) * rest)


def whole(shape):
    return pl.BlockSpec(tuple(shape), lambda i: (0,) * len(shape))


SCALARS = pl.BlockSpec(memory_space=pltpu.SMEM)


def call(kernel, images, ins, outs, scratch=(), flops=0):
    nbytes = sum(x.size * x.dtype.itemsize for x, _ in ins)
    shapes = [jax.ShapeDtypeStruct(shape, dtype) for shape, dtype, _ in outs]
    nbytes += sum(s.size * s.dtype.itemsize for s in shapes)
    return pl.pallas_call(
        kernel,
        grid=(images,),
        in_specs=[spec for _, spec in ins],
        out_specs=[spec for _, _, spec in outs],
        out_shape=shapes,
        scratch_shapes=list(scratch),
        compiler_params=kernel_params(),
        cost_estimate=cost(flops, nbytes),
    )(*[x for x, _ in ins])


def img(x):
    return (x, per_image(x.shape))


def all_(x):
    return (x, whole(x.shape))


def small_call(kernel, ins, shape):
    return pl.pallas_call(kernel, out_shape=jax.ShapeDtypeStruct(shape, F32))(*ins)


def weights_kernel(*refs):
    count = len(refs) // 5
    for k in range(count):
        k_ref = refs[k]
        ch = k_ref.shape[2]
        n = 3 * ch
        for turned in (False, True):
            out_ref, low_ref = refs[count + 4 * k + 2 * turned : count + 4 * k + 2 * turned + 2]
            for a in range(3):
                for c in range(3):
                    w = k_ref[2 - a, 2 - c].T if turned else k_ref[a, c]
                    high, low = split(w)
                    out_ref[a * ch : (a + 1) * ch, c * ch : (c + 1) * ch] = high
                    out_ref[a * ch : (a + 1) * ch, n + c * ch : n + (c + 1) * ch] = low
                    if a < 2:
                        low_ref[a * ch : (a + 1) * ch, c * ch : (c + 1) * ch] = high
                    else:
                        out_ref[3 * ch :, c * ch : (c + 1) * ch] = high
            out_ref[3 * ch :, n:] = jnp.zeros((ch, n), BF16)


def prepare(*kernels):
    ch = kernels[0].shape[2]
    shapes = [jax.ShapeDtypeStruct(s, BF16) for s in ((4 * ch, 6 * ch), (2 * ch, 3 * ch))]
    out = pl.pallas_call(
        weights_kernel, out_shape=shapes * (2 * len(kernels)), compiler_params=kernel_params()
    )(*kernels)
    return [out[2 * k : 2 * k + 2] for k in range(2 * len(kernels))]


def after(x, *others):
    return lax.optimization_barrier((x,) + others)[0]


def partner(x, axis, bit):
    return lax.ppermute(x, axis, [(k, k ^ bit) for k in range(lax.axis_size(axis))])


def bits(axis):
    return [1 << k for k in range(lax.axis_size(axis).bit_length() - 1)]


def far_bits():
    low, high = bits("rows")[-2:]
    return low, high, low + high


def gather_sums(x, join):
    for bit in bits("rows")[:-2]:
        x = join(x, partner(x, "rows", bit), bit)
    return jnp.stack([x] + [partner(x, "rows", bit) for bit in far_bits()])


def shift_rows(top_source, bottom_source):
    count = lax.axis_size("rows")
    forward = [(i, i + 1) for i in range(count - 1)]
    backward = [(b, a) for a, b in forward]
    return lax.ppermute(top_source, "rows", forward), lax.ppermute(bottom_source, "rows", backward)


def shift_bands(parts):
    row_devs, count = lax.axis_size("rows"), lax.axis_size("img")
    me = lax.axis_index("img")
    edge = jnp.concatenate([jnp.where(me == 0, p[:, :1], p[:, p.shape[1] - 1 :]) for p in parts], axis=2)
    edge = edge.reshape((count, -1) + edge.shape[1:])
    got = []
    for s in range(count):
        down, up = (count - 1 + s) % count, s
        block = lax.dynamic_index_in_dim(edge, jnp.where(me == 0, up, down), 0, keepdims=False)
        pairs = [(r * count + count - 1, (r + 1) * count + down) for r in range(row_devs - 1)]
        pairs += [(r * count, (r - 1) * count + up) for r in range(1, row_devs)]
        got.append(lax.ppermute(block, ("rows", "img"), pairs))
    got = jnp.stack(got)
    pick = lambda k: lax.dynamic_index_in_dim(got, k, 0, keepdims=False)
    return pick(lax.rem(me + 1, count)), pick(me)


def rotate_img(blocks):
    count = lax.axis_size("img")
    me = lax.axis_index("img")
    pick = lambda k: lax.dynamic_index_in_dim(blocks, lax.rem(k, count), 0, keepdims=False)
    came = [pick(me)]
    for d in range(1, count):
        came.append(lax.ppermute(pick(me + d), "img", [(k, (k + d) % count) for k in range(count)]))
    return came


def img_sources():
    count = lax.axis_size("img")
    me = lax.axis_index("img")
    return [lax.rem(me - d + count, count) for d in range(count)]


def slices(cols, shares):
    units, cuts, seen = cols // 8, [0], 0
    for share in shares[:-1]:
        seen += share
        cuts.append(8 * round(units * seen / sum(shares)))
    cuts.append(cols)
    return [(a, b) for a, b in zip(cuts, cuts[1:]) if b > a]


def swap_rows(x):
    return lax.all_to_all(x, "rows", 0, 0)


def trade(x, axis, bit):
    half = x.shape[0] // 2
    mine = lax.rem(lax.axis_index(axis) // bit, 2)
    keep = lax.dynamic_slice_in_dim(x, mine * half, half, 0)
    give = lax.dynamic_slice_in_dim(x, (1 - mine) * half, half, 0)
    return keep + partner(give, axis, bit)


def untrade(x, axis, bit):
    mine = lax.rem(lax.axis_index(axis) // bit, 2)
    other = partner(x, axis, bit)
    return jnp.where(mine == 0, jnp.concatenate([x, other]), jnp.concatenate([other, x]))


def far_place():
    return lax.axis_index("rows") // far_bits()[0]


def far_trade(x):
    quarter = x.shape[0] // 4
    part = lambda k: lax.dynamic_slice_in_dim(x, k * quarter, quarter, 0)
    place = far_place()
    kept = part(place)
    for d, bit in enumerate(far_bits()):
        kept = kept + partner(part(place ^ (d + 1)), "rows", bit)
    return kept


def far_untrade(x):
    parts = jnp.stack([x] + [partner(x, "rows", bit) for bit in far_bits()])
    place = far_place()
    return jnp.concatenate([lax.dynamic_index_in_dim(parts, place ^ k, 0, keepdims=False) for k in range(4)])


def shards(
    image_in, gain_one, shift_one, kernel_one, bias_one, gain_two, shift_two, kernel_two, bias_two, out_grad
):
    n, rows, cols, ch = image_in.shape
    local = rows * cols
    ext = rows + 2
    wide = cols + MARGIN
    place = lax.axis_index("rows")
    edge = jnp.stack([place > 0, place < lax.axis_size("rows") - 1]).astype(F32)
    edges = (edge, SCALARS)
    row_vec = lambda v: v[None, :]
    conv_flops = 2 * 9 * ch * ch * cols * 3 * n
    pair_shape = (2, n, ch)
    pair = (pair_shape, F32, whole(pair_shape))
    maps = lambda r: ((n, r, cols, ch), F32, per_image((n, r, cols, ch)))
    splits = lambda r: ((n, r, wide, 2 * ch), BF16, per_image((n, r, wide, 2 * ch)))
    taps = ((9, ch, ch), F32, whole((9, ch, ch)))
    row_devs, img_devs = lax.axis_size("rows"), lax.axis_size("img")
    slab = rows // img_devs
    in_cuts = slices(cols, (2, 5, 4))
    out_cuts = slices(cols, (3, 6, 2))
    me = lax.axis_index("img")
    norm = functools.partial(norm_kernel, local=local * row_devs // 4)
    back_norm = functools.partial(back_norm_kernel, local=local * row_devs // 4)
    back_norm_last = functools.partial(back_norm_kernel, local=local * row_devs)
    one_shape = (1, n, ch)
    one = (one_shape, F32, whole(one_shape))

    def join_spread(x, y, bit):
        off = x[0] - y[0]
        return jnp.stack([x[0] + y[0], x[1] + y[1] + off * off * (0.5 / (bit * local))])

    def join_add(x, y, bit):
        return x + y

    grad_in = out_grad.reshape(out_grad.shape[2:])
    landed, came = [], []

    def bring(k, *others):
        a, b = in_cuts[k]
        landed.append(swap_rows(after(grad_in[:, :, a:b], *others)))

    def settle(k, *others):
        a, b = in_cuts[k]
        came.append(rotate_img(after(landed[k], *others).reshape(img_devs, n, slab, b - a, ch)))

    w_one, w_one_back, w_two, w_two_back = prepare(kernel_one, kernel_two)

    top, bottom = shift_rows(image_in[:, rows - 2 :], image_in[:, :2])
    (stat_one,) = call(stats_kernel, n, [img(image_in)], [pair])
    bring(0, stat_one)
    far_one = after(gather_sums(stat_one, join_spread), landed[0], top, bottom)
    n_one = small_call(norm, (far_one, row_vec(gain_one), row_vec(shift_one)), (4, n, ch))
    bring(1, far_one)
    settle(0, far_one)
    middle, act_one, stat_two = call(
        conv_one_kernel,
        n,
        [edges, img(image_in), img(top), img(bottom), all_(n_one), *map(all_, w_one), all_(row_vec(bias_one))],
        [maps(ext), splits(ext), pair],
        [pltpu.VMEM((rows + 4, wide, 2 * ch), BF16)],
        conv_flops * ext,
    )
    far_two = after(gather_sums(after(stat_two, *came[0]), join_spread), landed[1])
    n_two = small_call(norm, (far_two, row_vec(gain_two), row_vec(shift_two)), (4, n, ch))
    bring(2, far_two)
    settle(1, far_two)
    banded_shape = (img_devs, n, slab, cols, ch)
    banded = (banded_shape, F32, pl.BlockSpec((img_devs, 1, slab, cols, ch), lambda i: (0, i, 0, 0, 0)))
    result, act_two = call(
        conv_two_kernel,
        n,
        [edges, img(middle), img(image_in), all_(n_two), *map(all_, w_two), all_(row_vec(bias_two))],
        [banded, splits(ext)],
        (),
        conv_flops * rows,
    )

    def turn(a, b, *others):
        bands = jnp.stack(rotate_img(after(result[..., a:b, :], *others)))
        pick = lambda j: lax.dynamic_index_in_dim(bands, lax.rem(me - j + img_devs, img_devs), 0, keepdims=False)
        return jnp.stack([pick(j) for j in range(img_devs)]).reshape(img_devs * n, slab, b - a, ch)

    mixed_parts = []

    def send(k, *others):
        mixed_parts.append(swap_rows(after(blocks[k], *others)))

    blocks = [turn(*out_cuts[0], *came[1])]
    cut = in_cuts[-1][0]
    offsets = tuple(a for a, _ in in_cuts)
    band = jnp.stack(img_sources()).astype(jnp.int32)

    def add_taps(before, act, parts, at, start, width, bands):
        return call(
            functools.partial(taps_kernel, offsets=tuple(at), start=start),
            n,
            [all_(before), img(act), (bands, SCALARS)] + [img(p) for line in parts for p in line],
            [taps, one],
            [pltpu.VMEM((rows, width, ch), F32), pltpu.VMEM((rows * width, 6 * ch), BF16)],
            conv_flops * rows * width / wide,
        )

    no_taps = jnp.zeros((9, ch, ch), F32)
    early, late = -(-(cut + 1) // 16) * 16, (cut - 1) // 16 * 16
    by_band = lambda parts: [[part[d] for part in parts] for d in range(img_devs)]
    taps_two, sum_early = add_taps(no_taps, act_two, by_band(came), offsets[:-1], 0, early, band)

    g_top, g_bottom = shift_bands(after(tuple(landed), result))
    settle(2, g_top, g_bottom, taps_two, blocks[0])
    blocks.append(turn(*out_cuts[1], *came[2]))
    blocks.append(turn(*out_cuts[2], blocks[1]))
    send(0, landed[2], blocks[0], g_top, g_bottom)
    grad_result, pre_two, sum_two = call(
        functools.partial(back_two_kernel, offsets=offsets),
        n,
        [(band, SCALARS), img(g_top), img(g_bottom), img(middle), all_(n_two), *map(all_, w_two_back)]
        + [img(p) for line in by_band(came) for p in line],
        [maps(rows), maps(rows), pair],
        [pltpu.VMEM((ext, wide, 2 * ch), BF16)],
        conv_flops * rows,
    )
    pre_top, pre_bottom = shift_rows(pre_two[:, rows - 1 :], pre_two[:, :1])
    far_back = after(gather_sums(sum_two, join_add), mixed_parts[0], blocks[1], pre_top, pre_bottom)
    b_two = small_call(back_norm, (far_back, n_two, row_vec(gain_two)), (5, n, ch))
    send(1, far_back)
    three = ((3, n, ch), F32, whole((3, n, ch)))
    grad_mid, partial, sum_one = call(
        back_one_kernel,
        n,
        [edges, img(pre_two), img(pre_top), img(pre_bottom), img(middle), all_(b_two), img(grad_result), img(image_in), all_(n_one), *map(all_, w_one_back)],
        [maps(rows), maps(rows), three],
        [pltpu.VMEM((ext, wide, 2 * ch), BF16)],
        conv_flops * rows,
    )
    taps_two, sum_late = add_taps(
        taps_two, after(act_two, b_two), by_band(came[-1:]), (cut - late,), late, wide - late, band
    )
    zero = jnp.zeros((1,), jnp.int32)
    taps_one, _ = add_taps(no_taps, after(act_one, blocks[2]), [[grad_mid]], (0,), 0, wide, zero)
    size = 9 * ch
    flat = jnp.concatenate([taps_one.reshape(size, ch), taps_two.reshape(size, ch)])
    steps = [("rows", k) for k in bits("rows")[:-2]] + [("img", k) for k in bits("img")]
    for axis, bit in steps:
        flat = trade(flat, axis, bit)
    sums = jnp.concatenate([sum_one, sum_early + sum_late], axis=0)
    for bit in bits("rows")[:-2]:
        sums = sums + partner(sums, "rows", bit)
    both = after(jnp.concatenate([sums.reshape(-1, ch), flat]), mixed_parts[1])
    both = both + sum(partner(both, "rows", bit) for bit in far_bits())
    far_last, flat = both[: sums.size // ch].reshape((1,) + sums.shape), both[sums.size // ch :]
    b_one = small_call(back_norm_last, (far_last, n_one, row_vec(gain_one)), (5, n, ch))
    empty = jnp.zeros((row_devs, slab, out_cuts[2][1] - out_cuts[2][0], ch), F32)
    mixed = jnp.concatenate(mixed_parts + [empty], axis=2)
    send(2, far_last, flat, mixed)
    (input_grad,) = call(final_kernel, n, [img(partial), img(image_in), all_(b_one)], [maps(rows)])
    for k, (axis, bit) in enumerate(reversed(steps)):
        flat = untrade(flat, axis, bit)
        if k == len(steps) - 2:
            flat = after(flat, input_grad)
    vectors = jnp.concatenate([jnp.sum(far_last, axis=(0, 2)), jnp.sum(far_back, axis=(0, 2))])
    for bit in bits("img"):
        vectors = vectors + partner(vectors, "img", bit)
    last = after(mixed_parts[-1], input_grad, flat, vectors)
    grad_kernel_one, grad_kernel_two = (k.reshape(3, 3, ch, ch) for k in (flat[:size], flat[size:]))
    mixed = lax.dynamic_update_slice_in_dim(mixed, last, out_cuts[2][0], 2)[None, None]
    return (
        mixed,
        input_grad,
        vectors[1],
        vectors[0],
        grad_kernel_one,
        vectors[2],
        vectors[5],
        vectors[4],
        grad_kernel_two,
        vectors[3],
    )


def solution(mesh):
    spread = P("img", "rows", None, None)
    banded = P("rows", "img", None, None, None, None)
    return jax.shard_map(
        shards,
        mesh=mesh,
        in_specs=(spread,) + (P(),) * 8 + (banded,),
        out_specs=(banded, spread) + (P(),) * 8,
        check_vma=False,
    )
```

```python
import functools

import jax
import jax.numpy as jnp
from jax import lax
from jax.experimental import pallas as pl
from jax.experimental.pallas import tpu as pltpu
from jax.sharding import PartitionSpec as P

GROUPS = 32
EPSILON = 1e-06
BF16 = jnp.bfloat16
F32 = jnp.float32
MARGIN = 8


def kernel_params():
    return pltpu.CompilerParams(vmem_limit_bytes=48 * 2**20)


def cost(flops, nbytes):
    return pl.CostEstimate(flops=int(flops) // 8, bytes_accessed=int(nbytes) // 8, transcendentals=0)


def split(x):
    high = x.astype(BF16)
    return high, (x - high.astype(F32)).astype(BF16)


def widen(x):
    return jnp.concatenate([x, jnp.zeros((x.shape[0], MARGIN, x.shape[2]), F32)], axis=1)


def put_split(s_ref, row, x):
    channels = x.shape[2]
    high, low = split(widen(x))
    s_ref[row : row + x.shape[0], :, 0:channels] = high
    s_ref[row : row + x.shape[0], :, channels:] = low


def conv_rows(s_ref, w_ref, low_ref, row, rows):
    wide, channels = s_ref.shape[1], s_ref.shape[2] // 2
    m, n = rows * wide, 3 * channels
    high = [s_ref[row + a : row + a + rows, :, 0:channels].reshape(m, channels) for a in range(3)]
    low = [s_ref[row + a : row + a + rows, :, channels:].reshape(m, channels) for a in range(3)]
    y = jnp.dot(jnp.concatenate(high + low[2:], axis=1), w_ref[...], preferred_element_type=F32)
    y = y[:, :n] + y[:, n:]
    y = y + jnp.dot(jnp.concatenate(low[:2], axis=1), low_ref[...], preferred_element_type=F32)
    out = y[:, channels : 2 * channels]
    out = out + pltpu.roll(y[:, :channels], 1, 0) + pltpu.roll(y[:, 2 * channels :], m - 1, 0)
    return out.reshape(rows, wide, channels)[:, : wide - MARGIN]


def row_blocks(total, size):
    return [(r, min(size, total - r)) for r in range(0, total, size)]


def silu(v):
    return v * jax.nn.sigmoid(v)


def silu_slope(v):
    s = jax.nn.sigmoid(v)
    return s * (1.0 + v * (1.0 - s))


def total(x):
    return jnp.sum(x.reshape(-1, x.shape[-1]), axis=0, keepdims=True)


def put_stats(out_ref, i, x):
    count = x.shape[0] * x.shape[1]
    added = total(x)
    mean = added * (1.0 / count)
    off = x - mean[None]
    out_ref[0, pl.ds(i, 1), :] = added
    out_ref[1, pl.ds(i, 1), :] = total(off * off)


def stats_kernel(x_ref, out_ref):
    put_stats(out_ref, pl.program_id(0), x_ref[0])


def conv_one_kernel(edge_ref, x_ref, top_ref, bot_ref, n_ref, w_ref, low_ref, b_ref, mid_ref, act_ref, stat_ref, s_ref):
    i = pl.program_id(0)
    rows = x_ref.shape[1]
    mean, scale, shift = n_ref[0, pl.ds(i, 1)], n_ref[1, pl.ds(i, 1)], n_ref[2, pl.ds(i, 1)]
    act = lambda v: silu((v - mean[None]) * scale[None] + shift[None])
    put_split(s_ref, 0, act(top_ref[0]) * edge_ref[0])
    put_split(s_ref, 2, act(x_ref[0]))
    put_split(s_ref, 2 + rows, act(bot_ref[0]) * edge_ref[1])
    act_ref[0] = s_ref[1 : rows + 3]
    for r, size in row_blocks(rows + 2, 6):
        mid_ref[0, r : r + size] = conv_rows(s_ref, w_ref, low_ref, r, size) + b_ref[...][None]
    put_stats(stat_ref, i, mid_ref[0, 1 : rows + 1])


def conv_two_kernel(edge_ref, mid_ref, x_ref, n_ref, w_ref, low_ref, b_ref, out_ref, act_ref):
    i = pl.program_id(0)
    rows = x_ref.shape[1]
    slab = out_ref.shape[2]
    mean, scale, shift = n_ref[0, pl.ds(i, 1)], n_ref[1, pl.ds(i, 1)], n_ref[2, pl.ds(i, 1)]
    act = lambda v: silu((v - mean[None]) * scale[None] + shift[None])
    s_ref = act_ref.at[0]
    put_split(s_ref, 0, act(mid_ref[0, 0:1]) * edge_ref[0])
    put_split(s_ref, 1, act(mid_ref[0, 1 : rows + 1]))
    put_split(s_ref, 1 + rows, act(mid_ref[0, rows + 1 :]) * edge_ref[1])
    for r, size in row_blocks(rows, slab):
        out_ref[r // slab, 0] = conv_rows(s_ref, w_ref, low_ref, r, size) + b_ref[...][None] + x_ref[0, r : r + size]


def back_two_kernel(band_ref, top_ref, bot_ref, mid_ref, n_ref, w_ref, low_ref, *refs, offsets):
    pieces, (g_ref, out_ref, sum_ref, s_ref) = refs[:-4], refs[-4:]
    i = pl.program_id(0)
    count = len(offsets)
    rows = g_ref.shape[1]
    mean, scale, shift, rstd = (n_ref[k, pl.ds(i, 1)][None] for k in range(4))
    for d in range(len(pieces) // count):
        for s, at in enumerate(offsets):
            piece = pieces[d * count + s]
            _, slab, cols, _ = piece.shape
            g_ref[0, pl.ds(band_ref[d] * slab, slab), at : at + cols, :] = piece[0]
    put_split(s_ref, 0, top_ref[0])
    put_split(s_ref, 1, g_ref[0])
    put_split(s_ref, 1 + rows, bot_ref[0])
    sums = [jnp.zeros((1, g_ref.shape[3]), F32)] * 2
    for r, size in row_blocks(rows, 8):
        off = mid_ref[0, r + 1 : r + 1 + size] - mean
        grad = conv_rows(s_ref, w_ref, low_ref, r, size) * silu_slope(off * scale + shift)
        out_ref[0, r : r + size] = grad
        sums = [sums[0] + total(grad), sums[1] + total(grad * (off * rstd))]
    sum_ref[0, pl.ds(i, 1), :] = sums[0]
    sum_ref[1, pl.ds(i, 1), :] = sums[1]


def taps_kernel(before_ref, act_ref, *refs, offsets, start):
    band_ref, pieces, (out_ref, sum_ref, g_ref, g_scr) = refs[0], refs[1:-4], refs[-4:]
    channels = g_ref.shape[2]
    rows, width, _ = g_ref.shape
    m = rows * width
    i = pl.program_id(0)

    @pl.when(i == 0)
    def _():
        out_ref[...] = before_ref[...]
        g_ref[...] = jnp.zeros_like(g_ref)

    count = len(offsets)
    for k in range(len(pieces) // count):
        for s, at in enumerate(offsets):
            piece = pieces[k * count + s]
            _, slab, cols, _ = piece.shape
            g_ref[pl.ds(band_ref[k] * slab, slab), at : at + cols, :] = piece[0]
    flat = g_ref[...].reshape(m, channels)
    sum_ref[0, pl.ds(i, 1), :] = total(flat)
    column = lax.broadcasted_iota(jnp.int32, (rows, width, channels), 1).reshape(m, channels)
    right = jnp.where(column < width - 1, pltpu.roll(flat, m - 1, 0), 0.0)
    for c, shifted in enumerate((right, flat, pltpu.roll(flat, 1, 0))):
        high, low = split(shifted)
        g_scr[:, c * channels : (c + 1) * channels] = high
        g_scr[:, (c + 3) * channels : (c + 4) * channels] = low
    over_pixels = (((0,), (0,)), ((), ()))
    n = 3 * channels
    for a in range(3):
        high = act_ref[0, a : a + rows, start : start + width, 0:channels].reshape(m, channels)
        low = act_ref[0, a : a + rows, start : start + width, channels:].reshape(m, channels)
        p = lax.dot_general(high, g_scr[...], over_pixels, preferred_element_type=F32)
        q = lax.dot_general(low, g_scr[:, :n], over_pixels, preferred_element_type=F32)
        both = p[:, :n] + p[:, n:] + q
        for c in range(3):
            out_ref[3 * a + c] += both[:, c * channels : (c + 1) * channels]


def back_one_kernel(edge_ref, pre_ref, top_ref, bot_ref, mid_ref, b_ref, g_ref, x_ref, n_ref, w_ref, low_ref, gm_ref, out_ref, sum_ref, s_ref):
    i = pl.program_id(0)
    rows = x_ref.shape[1]
    mid_mean, mid_rstd, gain, first, second = (b_ref[k, pl.ds(i, 1)][None] for k in range(5))
    mean, scale, shift, rstd = (n_ref[k, pl.ds(i, 1)][None] for k in range(4))

    def back(pre, mid):
        normed = (mid - mid_mean) * mid_rstd
        return mid_rstd * (pre * gain - first - normed * second)

    own = back(pre_ref[0], mid_ref[0, 1 : rows + 1])
    gm_ref[0] = own
    put_split(s_ref, 0, back(top_ref[0], mid_ref[0, 0:1]) * edge_ref[0])
    put_split(s_ref, 1, own)
    put_split(s_ref, 1 + rows, back(bot_ref[0], mid_ref[0, rows + 1 :]) * edge_ref[1])
    sum_ref[2, pl.ds(i, 1), :] = total(own)
    sums = [jnp.zeros((1, x_ref.shape[3]), F32)] * 2
    for r, size in row_blocks(rows, 8):
        off = x_ref[0, r : r + size] - mean
        grad = conv_rows(s_ref, w_ref, low_ref, r, size) * silu_slope(off * scale + shift)
        out_ref[0, r : r + size] = g_ref[0, r : r + size] + scale * grad
        sums = [sums[0] + total(grad), sums[1] + total(grad * (off * rstd))]
    sum_ref[0, pl.ds(i, 1), :] = sums[0]
    sum_ref[1, pl.ds(i, 1), :] = sums[1]


def final_kernel(u_ref, x_ref, n_ref, out_ref):
    i = pl.program_id(0)
    mean, rstd, _, first, second = (n_ref[k, pl.ds(i, 1)][None] for k in range(5))
    out_ref[0] = u_ref[0] - rstd * (first + (x_ref[0] - mean) * rstd * second)


def same_group(channels):
    width = channels // GROUPS
    row = lax.broadcasted_iota(jnp.int32, (channels, channels), 0) // width
    col = lax.broadcasted_iota(jnp.int32, (channels, channels), 1) // width
    return (row == col).astype(F32)


def over_group(x):
    return jnp.dot(x, same_group(x.shape[-1]), precision=lax.Precision.HIGHEST, preferred_element_type=F32)


def norm_kernel(all_ref, gain_ref, shift_ref, out_ref, *, local):
    devices, _, _, channels = all_ref.shape
    count = devices * local * (channels // GROUPS)
    added = all_ref[:, 0]
    mean = over_group(jnp.sum(added, axis=0)) * (1.0 / count)
    off = added * (1.0 / local) - mean[None]
    spread = over_group(jnp.sum(all_ref[:, 1] + off * off * float(local), axis=0)) * (1.0 / count)
    rstd = lax.rsqrt(spread + EPSILON)
    out_ref[0] = mean
    out_ref[1] = rstd * gain_ref[...]
    out_ref[2] = jnp.broadcast_to(shift_ref[...], mean.shape)
    out_ref[3] = rstd


def back_norm_kernel(all_ref, n_ref, gain_ref, out_ref, *, local):
    devices, _, _, channels = all_ref.shape
    count = devices * local * (channels // GROUPS)
    out_ref[0] = n_ref[0]
    out_ref[1] = n_ref[3]
    out_ref[2] = jnp.broadcast_to(gain_ref[...], n_ref[0].shape)
    for k in range(2):
        out_ref[3 + k] = over_group(jnp.sum(all_ref[:, k], axis=0) * gain_ref[...]) * (1.0 / count)


def per_image(shape):
    rest = len(shape) - 1
    return pl.BlockSpec((1,) + tuple(shape[1:]), lambda i: (i,) + (0,) * rest)


def whole(shape):
    return pl.BlockSpec(tuple(shape), lambda i: (0,) * len(shape))


SCALARS = pl.BlockSpec(memory_space=pltpu.SMEM)


def call(kernel, images, ins, outs, scratch=(), flops=0):
    nbytes = sum(x.size * x.dtype.itemsize for x, _ in ins)
    shapes = [jax.ShapeDtypeStruct(shape, dtype) for shape, dtype, _ in outs]
    nbytes += sum(s.size * s.dtype.itemsize for s in shapes)
    return pl.pallas_call(
        kernel,
        grid=(images,),
        in_specs=[spec for _, spec in ins],
        out_specs=[spec for _, _, spec in outs],
        out_shape=shapes,
        scratch_shapes=list(scratch),
        compiler_params=kernel_params(),
        cost_estimate=cost(flops, nbytes),
    )(*[x for x, _ in ins])


def img(x):
    return (x, per_image(x.shape))


def all_(x):
    return (x, whole(x.shape))


def small_call(kernel, ins, shape):
    return pl.pallas_call(kernel, out_shape=jax.ShapeDtypeStruct(shape, F32))(*ins)


def weights_kernel(*refs):
    count = len(refs) // 5
    for k in range(count):
        k_ref = refs[k]
        ch = k_ref.shape[2]
        n = 3 * ch
        for turned in (False, True):
            out_ref, low_ref = refs[count + 4 * k + 2 * turned : count + 4 * k + 2 * turned + 2]
            for a in range(3):
                for c in range(3):
                    w = k_ref[2 - a, 2 - c].T if turned else k_ref[a, c]
                    high, low = split(w)
                    out_ref[a * ch : (a + 1) * ch, c * ch : (c + 1) * ch] = high
                    out_ref[a * ch : (a + 1) * ch, n + c * ch : n + (c + 1) * ch] = low
                    if a < 2:
                        low_ref[a * ch : (a + 1) * ch, c * ch : (c + 1) * ch] = high
                    else:
                        out_ref[3 * ch :, c * ch : (c + 1) * ch] = high
            out_ref[3 * ch :, n:] = jnp.zeros((ch, n), BF16)


def prepare(*kernels):
    ch = kernels[0].shape[2]
    shapes = [jax.ShapeDtypeStruct(s, BF16) for s in ((4 * ch, 6 * ch), (2 * ch, 3 * ch))]
    out = pl.pallas_call(
        weights_kernel, out_shape=shapes * (2 * len(kernels)), compiler_params=kernel_params()
    )(*kernels)
    return [out[2 * k : 2 * k + 2] for k in range(2 * len(kernels))]


def after(x, *others):
    return lax.optimization_barrier((x,) + others)[0]


def partner(x, axis, bit):
    return lax.ppermute(x, axis, [(k, k ^ bit) for k in range(lax.axis_size(axis))])


def bits(axis):
    return [1 << k for k in range(lax.axis_size(axis).bit_length() - 1)]


def far_bits():
    low, high = bits("rows")[-2:]
    return low, high, low + high


def gather_sums(x, join):
    for bit in bits("rows")[:-2]:
        x = join(x, partner(x, "rows", bit), bit)
    return jnp.stack([x] + [partner(x, "rows", bit) for bit in far_bits()])


def shift_rows(top_source, bottom_source):
    count = lax.axis_size("rows")
    forward = [(i, i + 1) for i in range(count - 1)]
    backward = [(b, a) for a, b in forward]
    return lax.ppermute(top_source, "rows", forward), lax.ppermute(bottom_source, "rows", backward)


def shift_bands(parts):
    row_devs, count = lax.axis_size("rows"), lax.axis_size("img")
    me = lax.axis_index("img")
    edge = jnp.concatenate([jnp.where(me == 0, p[:, :1], p[:, p.shape[1] - 1 :]) for p in parts], axis=2)
    edge = edge.reshape((count, -1) + edge.shape[1:])
    got = []
    for s in range(count):
        down, up = (count - 1 + s) % count, s
        block = lax.dynamic_index_in_dim(edge, jnp.where(me == 0, up, down), 0, keepdims=False)
        pairs = [(r * count + count - 1, (r + 1) * count + down) for r in range(row_devs - 1)]
        pairs += [(r * count, (r - 1) * count + up) for r in range(1, row_devs)]
        got.append(lax.ppermute(block, ("rows", "img"), pairs))
    got = jnp.stack(got)
    pick = lambda k: lax.dynamic_index_in_dim(got, k, 0, keepdims=False)
    return pick(lax.rem(me + 1, count)), pick(me)


def rotate_img(blocks):
    count = lax.axis_size("img")
    me = lax.axis_index("img")
    pick = lambda k: lax.dynamic_index_in_dim(blocks, lax.rem(k, count), 0, keepdims=False)
    came = [pick(me)]
    for d in range(1, count):
        came.append(lax.ppermute(pick(me + d), "img", [(k, (k + d) % count) for k in range(count)]))
    return came


def img_sources():
    count = lax.axis_size("img")
    me = lax.axis_index("img")
    return [lax.rem(me - d + count, count) for d in range(count)]


def slices(cols, shares):
    units, cuts, seen = cols // 8, [0], 0
    for share in shares[:-1]:
        seen += share
        cuts.append(8 * round(units * seen / sum(shares)))
    cuts.append(cols)
    return [(a, b) for a, b in zip(cuts, cuts[1:]) if b > a]


def swap_rows(x):
    return lax.all_to_all(x, "rows", 0, 0)


def trade(x, axis, bit):
    half = x.shape[0] // 2
    mine = lax.rem(lax.axis_index(axis) // bit, 2)
    keep = lax.dynamic_slice_in_dim(x, mine * half, half, 0)
    give = lax.dynamic_slice_in_dim(x, (1 - mine) * half, half, 0)
    return keep + partner(give, axis, bit)


def untrade(x, axis, bit):
    mine = lax.rem(lax.axis_index(axis) // bit, 2)
    other = partner(x, axis, bit)
    return jnp.where(mine == 0, jnp.concatenate([x, other]), jnp.concatenate([other, x]))


def far_place():
    return lax.axis_index("rows") // far_bits()[0]


def far_trade(x):
    quarter = x.shape[0] // 4
    part = lambda k: lax.dynamic_slice_in_dim(x, k * quarter, quarter, 0)
    place = far_place()
    kept = part(place)
    for d, bit in enumerate(far_bits()):
        kept = kept + partner(part(place ^ (d + 1)), "rows", bit)
    return kept


def far_untrade(x):
    parts = jnp.stack([x] + [partner(x, "rows", bit) for bit in far_bits()])
    place = far_place()
    return jnp.concatenate([lax.dynamic_index_in_dim(parts, place ^ k, 0, keepdims=False) for k in range(4)])


def shards(
    image_in, gain_one, shift_one, kernel_one, bias_one, gain_two, shift_two, kernel_two, bias_two, out_grad
):
    n, rows, cols, ch = image_in.shape
    local = rows * cols
    ext = rows + 2
    wide = cols + MARGIN
    place = lax.axis_index("rows")
    edge = jnp.stack([place > 0, place < lax.axis_size("rows") - 1]).astype(F32)
    edges = (edge, SCALARS)
    row_vec = lambda v: v[None, :]
    conv_flops = 2 * 9 * ch * ch * cols * 3 * n
    pair_shape = (2, n, ch)
    pair = (pair_shape, F32, whole(pair_shape))
    maps = lambda r: ((n, r, cols, ch), F32, per_image((n, r, cols, ch)))
    splits = lambda r: ((n, r, wide, 2 * ch), BF16, per_image((n, r, wide, 2 * ch)))
    taps = ((9, ch, ch), F32, whole((9, ch, ch)))
    row_devs, img_devs = lax.axis_size("rows"), lax.axis_size("img")
    slab = rows // img_devs
    in_cuts = slices(cols, (3, 4, 4))
    out_cuts = slices(cols, (3, 6, 2))
    me = lax.axis_index("img")
    norm = functools.partial(norm_kernel, local=local * row_devs // 4)
    back_norm = functools.partial(back_norm_kernel, local=local * row_devs // 4)
    back_norm_last = functools.partial(back_norm_kernel, local=local * row_devs)
    one_shape = (1, n, ch)
    one = (one_shape, F32, whole(one_shape))

    def join_spread(x, y, bit):
        off = x[0] - y[0]
        return jnp.stack([x[0] + y[0], x[1] + y[1] + off * off * (0.5 / (bit * local))])

    def join_add(x, y, bit):
        return x + y

    grad_in = out_grad.reshape(out_grad.shape[2:])
    landed, came = [], []

    def bring(k, *others):
        a, b = in_cuts[k]
        landed.append(swap_rows(after(grad_in[:, :, a:b], *others)))

    def settle(k, *others):
        a, b = in_cuts[k]
        came.append(rotate_img(after(landed[k], *others).reshape(img_devs, n, slab, b - a, ch)))

    w_one, w_one_back, w_two, w_two_back = prepare(kernel_one, kernel_two)

    top, bottom = shift_rows(image_in[:, rows - 2 :], image_in[:, :2])
    (stat_one,) = call(stats_kernel, n, [img(image_in)], [pair])
    bring(0, stat_one)
    far_one = after(gather_sums(stat_one, join_spread), landed[0], top, bottom)
    n_one = small_call(norm, (far_one, row_vec(gain_one), row_vec(shift_one)), (4, n, ch))
    bring(1, far_one)
    settle(0, far_one)
    middle, act_one, stat_two = call(
        conv_one_kernel,
        n,
        [edges, img(image_in), img(top), img(bottom), all_(n_one), *map(all_, w_one), all_(row_vec(bias_one))],
        [maps(ext), splits(ext), pair],
        [pltpu.VMEM((rows + 4, wide, 2 * ch), BF16)],
        conv_flops * ext,
    )
    far_two = after(gather_sums(after(stat_two, *came[0]), join_spread), landed[1])
    n_two = small_call(norm, (far_two, row_vec(gain_two), row_vec(shift_two)), (4, n, ch))
    bring(2, far_two)
    settle(1, far_two)
    banded_shape = (img_devs, n, slab, cols, ch)
    banded = (banded_shape, F32, pl.BlockSpec((img_devs, 1, slab, cols, ch), lambda i: (0, i, 0, 0, 0)))
    result, act_two = call(
        conv_two_kernel,
        n,
        [edges, img(middle), img(image_in), all_(n_two), *map(all_, w_two), all_(row_vec(bias_two))],
        [banded, splits(ext)],
        (),
        conv_flops * rows,
    )

    def turn(a, b, *others):
        bands = jnp.stack(rotate_img(after(result[..., a:b, :], *others)))
        pick = lambda j: lax.dynamic_index_in_dim(bands, lax.rem(me - j + img_devs, img_devs), 0, keepdims=False)
        return jnp.stack([pick(j) for j in range(img_devs)]).reshape(img_devs * n, slab, b - a, ch)

    mixed_parts = []

    def send(k, *others):
        mixed_parts.append(swap_rows(after(blocks[k], *others)))

    blocks = [turn(*out_cuts[0], *came[1])]
    cut = in_cuts[-1][0]
    offsets = tuple(a for a, _ in in_cuts)
    band = jnp.stack(img_sources()).astype(jnp.int32)

    def add_taps(before, act, parts, at, start, width, bands):
        act_in = img(act)
        if start % width == 0:
            place, start = start // width, 0
            act_in = (act, pl.BlockSpec((1, ext, width, 2 * ch), lambda i: (i, 0, place, 0)))
        return call(
            functools.partial(taps_kernel, offsets=tuple(at), start=start),
            n,
            [all_(before), act_in, (bands, SCALARS)] + [img(p) for line in parts for p in line],
            [taps, one],
            [pltpu.VMEM((rows, width, ch), F32), pltpu.VMEM((rows * width, 6 * ch), BF16)],
            conv_flops * rows * width / wide,
        )

    no_taps = jnp.zeros((9, ch, ch), F32)
    early, late = -(-(cut + 1) // 16) * 16, (cut - 1) // 16 * 16
    by_band = lambda parts: [[part[d] for part in parts] for d in range(img_devs)]
    taps_two, sum_early = add_taps(no_taps, act_two, by_band(came), offsets[:-1], 0, early, band)

    g_top, g_bottom = shift_bands(after(tuple(landed), result))
    settle(2, g_top, g_bottom, blocks[0])
    blocks.append(turn(*out_cuts[1], *came[2]))
    blocks.append(turn(*out_cuts[2], blocks[1]))
    send(0, landed[2], blocks[0], g_top, g_bottom, taps_two)
    grad_result, pre_two, sum_two = call(
        functools.partial(back_two_kernel, offsets=offsets),
        n,
        [(band, SCALARS), img(g_top), img(g_bottom), img(middle), all_(n_two), *map(all_, w_two_back)]
        + [img(p) for line in by_band(came) for p in line],
        [maps(rows), maps(rows), pair],
        [pltpu.VMEM((ext, wide, 2 * ch), BF16)],
        conv_flops * rows,
    )
    pre_top, pre_bottom = shift_rows(pre_two[:, rows - 1 :], pre_two[:, :1])
    far_back = after(gather_sums(sum_two, join_add), mixed_parts[0], blocks[1], pre_top, pre_bottom)
    b_two = small_call(back_norm, (far_back, n_two, row_vec(gain_two)), (5, n, ch))
    send(1, far_back)
    three = ((3, n, ch), F32, whole((3, n, ch)))
    grad_mid, partial, sum_one = call(
        back_one_kernel,
        n,
        [edges, img(pre_two), img(pre_top), img(pre_bottom), img(middle), all_(b_two), img(grad_result), img(image_in), all_(n_one), *map(all_, w_one_back)],
        [maps(rows), maps(rows), three],
        [pltpu.VMEM((ext, wide, 2 * ch), BF16)],
        conv_flops * rows,
    )
    taps_two, sum_late = add_taps(
        taps_two, after(act_two, b_two), by_band(came[-1:]), (cut - late,), late, wide - late, band
    )
    zero = jnp.zeros((1,), jnp.int32)
    taps_one, _ = add_taps(no_taps, after(act_one, blocks[2]), [[grad_mid]], (0,), 0, wide, zero)
    size = 9 * ch
    flat = jnp.concatenate([taps_one.reshape(size, ch), taps_two.reshape(size, ch)])
    steps = [("rows", k) for k in bits("rows")[:-2]] + [("img", k) for k in bits("img")]
    for axis, bit in steps:
        flat = trade(flat, axis, bit)
    sums = jnp.concatenate([sum_one, sum_early + sum_late], axis=0)
    for bit in bits("rows")[:-2]:
        sums = sums + partner(sums, "rows", bit)
    both = after(jnp.concatenate([sums.reshape(-1, ch), flat]), mixed_parts[1])
    both = both + sum(partner(both, "rows", bit) for bit in far_bits())
    far_last, flat = both[: sums.size // ch].reshape((1,) + sums.shape), both[sums.size // ch :]
    b_one = small_call(back_norm_last, (far_last, n_one, row_vec(gain_one)), (5, n, ch))
    empty = jnp.zeros((row_devs, slab, out_cuts[2][1] - out_cuts[2][0], ch), F32)
    mixed = jnp.concatenate(mixed_parts + [empty], axis=2)
    send(2, far_last, flat, mixed)
    (input_grad,) = call(final_kernel, n, [img(partial), img(image_in), all_(b_one)], [maps(rows)])
    for k, (axis, bit) in enumerate(reversed(steps)):
        flat = untrade(flat, axis, bit)
        if k == len(steps) - 1:
            flat = after(flat, input_grad)
    vectors = jnp.concatenate([jnp.sum(far_last, axis=(0, 2)), jnp.sum(far_back, axis=(0, 2))])
    for bit in bits("img"):
        vectors = vectors + partner(vectors, "img", bit)
    last = after(mixed_parts[-1], input_grad, flat, vectors)
    grad_kernel_one, grad_kernel_two = (k.reshape(3, 3, ch, ch) for k in (flat[:size], flat[size:]))
    mixed = lax.dynamic_update_slice_in_dim(mixed, last, out_cuts[2][0], 2)[None, None]
    return (
        mixed,
        input_grad,
        vectors[1],
        vectors[0],
        grad_kernel_one,
        vectors[2],
        vectors[5],
        vectors[4],
        grad_kernel_two,
        vectors[3],
    )


def solution(mesh):
    spread = P("img", "rows", None, None)
    banded = P("rows", "img", None, None, None, None)
    return jax.shard_map(
        shards,
        mesh=mesh,
        in_specs=(spread,) + (P(),) * 8 + (banded,),
        out_specs=(banded, spread) + (P(),) * 8,
        check_vma=False,
    )
```

```python
import functools

import jax
import jax.numpy as jnp
from jax import lax
from jax.experimental import pallas as pl
from jax.experimental.pallas import tpu as pltpu
from jax.sharding import PartitionSpec as P

GROUPS = 32
EPSILON = 1e-06
BF16 = jnp.bfloat16
F32 = jnp.float32
MARGIN = 8


def kernel_params():
    return pltpu.CompilerParams(vmem_limit_bytes=48 * 2**20)


def cost(flops, nbytes):
    return pl.CostEstimate(flops=int(flops) // 8, bytes_accessed=int(nbytes) // 8, transcendentals=0)


def split(x):
    high = x.astype(BF16)
    return high, (x - high.astype(F32)).astype(BF16)


def widen(x):
    return jnp.concatenate([x, jnp.zeros((x.shape[0], MARGIN, x.shape[2]), F32)], axis=1)


def put_split(s_ref, row, x):
    channels = x.shape[2]
    high, low = split(widen(x))
    s_ref[row : row + x.shape[0], :, 0:channels] = high
    s_ref[row : row + x.shape[0], :, channels:] = low


def conv_rows(s_ref, w_ref, low_ref, row, rows):
    wide, channels = s_ref.shape[1], s_ref.shape[2] // 2
    m, n = rows * wide, 3 * channels
    high = [s_ref[row + a : row + a + rows, :, 0:channels].reshape(m, channels) for a in range(3)]
    low = [s_ref[row + a : row + a + rows, :, channels:].reshape(m, channels) for a in range(3)]
    y = jnp.dot(jnp.concatenate(high + low[2:], axis=1), w_ref[...], preferred_element_type=F32)
    y = y[:, :n] + y[:, n:]
    y = y + jnp.dot(jnp.concatenate(low[:2], axis=1), low_ref[...], preferred_element_type=F32)
    out = y[:, channels : 2 * channels]
    out = out + pltpu.roll(y[:, :channels], 1, 0) + pltpu.roll(y[:, 2 * channels :], m - 1, 0)
    return out.reshape(rows, wide, channels)[:, : wide - MARGIN]


def row_blocks(total, size):
    return [(r, min(size, total - r)) for r in range(0, total, size)]


def silu(v):
    return v * jax.nn.sigmoid(v)


def silu_slope(v):
    s = jax.nn.sigmoid(v)
    return s * (1.0 + v * (1.0 - s))


def total(x):
    return jnp.sum(x.reshape(-1, x.shape[-1]), axis=0, keepdims=True)


def put_stats(out_ref, i, x):
    count = x.shape[0] * x.shape[1]
    added = total(x)
    mean = added * (1.0 / count)
    off = x - mean[None]
    out_ref[0, pl.ds(i, 1), :] = added
    out_ref[1, pl.ds(i, 1), :] = total(off * off)


def stats_kernel(x_ref, out_ref):
    put_stats(out_ref, pl.program_id(0), x_ref[0])


def conv_one_kernel(edge_ref, x_ref, top_ref, bot_ref, n_ref, w_ref, low_ref, b_ref, mid_ref, act_ref, stat_ref, s_ref):
    i = pl.program_id(0)
    rows = x_ref.shape[1]
    mean, scale, shift = n_ref[0, pl.ds(i, 1)], n_ref[1, pl.ds(i, 1)], n_ref[2, pl.ds(i, 1)]
    act = lambda v: silu((v - mean[None]) * scale[None] + shift[None])
    put_split(s_ref, 0, act(top_ref[0]) * edge_ref[0])
    put_split(s_ref, 2, act(x_ref[0]))
    put_split(s_ref, 2 + rows, act(bot_ref[0]) * edge_ref[1])
    act_ref[0] = s_ref[1 : rows + 3]
    for r, size in row_blocks(rows + 2, 6):
        mid_ref[0, r : r + size] = conv_rows(s_ref, w_ref, low_ref, r, size) + b_ref[...][None]
    put_stats(stat_ref, i, mid_ref[0, 1 : rows + 1])


def conv_two_kernel(edge_ref, mid_ref, x_ref, n_ref, w_ref, low_ref, b_ref, out_ref, act_ref):
    i = pl.program_id(0)
    rows = x_ref.shape[1]
    slab = out_ref.shape[2]
    mean, scale, shift = n_ref[0, pl.ds(i, 1)], n_ref[1, pl.ds(i, 1)], n_ref[2, pl.ds(i, 1)]
    act = lambda v: silu((v - mean[None]) * scale[None] + shift[None])
    s_ref = act_ref.at[0]
    put_split(s_ref, 0, act(mid_ref[0, 0:1]) * edge_ref[0])
    put_split(s_ref, 1, act(mid_ref[0, 1 : rows + 1]))
    put_split(s_ref, 1 + rows, act(mid_ref[0, rows + 1 :]) * edge_ref[1])
    for r, size in row_blocks(rows, slab):
        out_ref[r // slab, 0] = conv_rows(s_ref, w_ref, low_ref, r, size) + b_ref[...][None] + x_ref[0, r : r + size]


def back_two_kernel(band_ref, top_ref, bot_ref, mid_ref, n_ref, w_ref, low_ref, *refs, offsets):
    pieces, (g_ref, out_ref, sum_ref, s_ref) = refs[:-4], refs[-4:]
    i = pl.program_id(0)
    count = len(offsets)
    rows = g_ref.shape[1]
    mean, scale, shift, rstd = (n_ref[k, pl.ds(i, 1)][None] for k in range(4))
    for d in range(len(pieces) // count):
        for s, at in enumerate(offsets):
            piece = pieces[d * count + s]
            _, slab, cols, _ = piece.shape
            g_ref[0, pl.ds(band_ref[d] * slab, slab), at : at + cols, :] = piece[0]
    put_split(s_ref, 0, top_ref[0])
    put_split(s_ref, 1, g_ref[0])
    put_split(s_ref, 1 + rows, bot_ref[0])
    sums = [jnp.zeros((1, g_ref.shape[3]), F32)] * 2
    for r, size in row_blocks(rows, 8):
        off = mid_ref[0, r + 1 : r + 1 + size] - mean
        grad = conv_rows(s_ref, w_ref, low_ref, r, size) * silu_slope(off * scale + shift)
        out_ref[0, r : r + size] = grad
        sums = [sums[0] + total(grad), sums[1] + total(grad * (off * rstd))]
    sum_ref[0, pl.ds(i, 1), :] = sums[0]
    sum_ref[1, pl.ds(i, 1), :] = sums[1]


def taps_kernel(before_ref, act_ref, *refs, offsets, start):
    band_ref, pieces, (out_ref, sum_ref, g_ref, g_scr) = refs[0], refs[1:-4], refs[-4:]
    channels = g_ref.shape[2]
    rows, width, _ = g_ref.shape
    m = rows * width
    i = pl.program_id(0)

    @pl.when(i == 0)
    def _():
        out_ref[...] = before_ref[...]
        g_ref[...] = jnp.zeros_like(g_ref)

    count = len(offsets)
    for k in range(len(pieces) // count):
        for s, at in enumerate(offsets):
            piece = pieces[k * count + s]
            _, slab, cols, _ = piece.shape
            g_ref[pl.ds(band_ref[k] * slab, slab), at : at + cols, :] = piece[0]
    flat = g_ref[...].reshape(m, channels)
    sum_ref[0, pl.ds(i, 1), :] = total(flat)
    column = lax.broadcasted_iota(jnp.int32, (rows, width, channels), 1).reshape(m, channels)
    right = jnp.where(column < width - 1, pltpu.roll(flat, m - 1, 0), 0.0)
    for c, shifted in enumerate((right, flat, pltpu.roll(flat, 1, 0))):
        high, low = split(shifted)
        g_scr[:, c * channels : (c + 1) * channels] = high
        g_scr[:, (c + 3) * channels : (c + 4) * channels] = low
    over_pixels = (((0,), (0,)), ((), ()))
    n = 3 * channels
    for a in range(3):
        high = act_ref[0, a : a + rows, start : start + width, 0:channels].reshape(m, channels)
        low = act_ref[0, a : a + rows, start : start + width, channels:].reshape(m, channels)
        p = lax.dot_general(high, g_scr[...], over_pixels, preferred_element_type=F32)
        q = lax.dot_general(low, g_scr[:, :n], over_pixels, preferred_element_type=F32)
        both = p[:, :n] + p[:, n:] + q
        for c in range(3):
            out_ref[3 * a + c] += both[:, c * channels : (c + 1) * channels]


def back_one_kernel(edge_ref, pre_ref, top_ref, bot_ref, mid_ref, b_ref, g_ref, x_ref, n_ref, w_ref, low_ref, gm_ref, out_ref, sum_ref, s_ref):
    i = pl.program_id(0)
    rows = x_ref.shape[1]
    mid_mean, mid_rstd, gain, first, second = (b_ref[k, pl.ds(i, 1)][None] for k in range(5))
    mean, scale, shift, rstd = (n_ref[k, pl.ds(i, 1)][None] for k in range(4))

    def back(pre, mid):
        normed = (mid - mid_mean) * mid_rstd
        return mid_rstd * (pre * gain - first - normed * second)

    own = back(pre_ref[0], mid_ref[0, 1 : rows + 1])
    gm_ref[0] = own
    put_split(s_ref, 0, back(top_ref[0], mid_ref[0, 0:1]) * edge_ref[0])
    put_split(s_ref, 1, own)
    put_split(s_ref, 1 + rows, back(bot_ref[0], mid_ref[0, rows + 1 :]) * edge_ref[1])
    sum_ref[2, pl.ds(i, 1), :] = total(own)
    sums = [jnp.zeros((1, x_ref.shape[3]), F32)] * 2
    for r, size in row_blocks(rows, 8):
        off = x_ref[0, r : r + size] - mean
        grad = conv_rows(s_ref, w_ref, low_ref, r, size) * silu_slope(off * scale + shift)
        out_ref[0, r : r + size] = g_ref[0, r : r + size] + scale * grad
        sums = [sums[0] + total(grad), sums[1] + total(grad * (off * rstd))]
    sum_ref[0, pl.ds(i, 1), :] = sums[0]
    sum_ref[1, pl.ds(i, 1), :] = sums[1]


def final_kernel(u_ref, x_ref, n_ref, out_ref):
    i = pl.program_id(0)
    mean, rstd, _, first, second = (n_ref[k, pl.ds(i, 1)][None] for k in range(5))
    out_ref[0] = u_ref[0] - rstd * (first + (x_ref[0] - mean) * rstd * second)


def same_group(channels):
    width = channels // GROUPS
    row = lax.broadcasted_iota(jnp.int32, (channels, channels), 0) // width
    col = lax.broadcasted_iota(jnp.int32, (channels, channels), 1) // width
    return (row == col).astype(F32)


def over_group(x):
    return jnp.dot(x, same_group(x.shape[-1]), precision=lax.Precision.HIGHEST, preferred_element_type=F32)


def norm_kernel(all_ref, gain_ref, shift_ref, out_ref, *, local):
    devices, _, _, channels = all_ref.shape
    count = devices * local * (channels // GROUPS)
    added = all_ref[:, 0]
    mean = over_group(jnp.sum(added, axis=0)) * (1.0 / count)
    off = added * (1.0 / local) - mean[None]
    spread = over_group(jnp.sum(all_ref[:, 1] + off * off * float(local), axis=0)) * (1.0 / count)
    rstd = lax.rsqrt(spread + EPSILON)
    out_ref[0] = mean
    out_ref[1] = rstd * gain_ref[...]
    out_ref[2] = jnp.broadcast_to(shift_ref[...], mean.shape)
    out_ref[3] = rstd


def back_norm_kernel(all_ref, n_ref, gain_ref, out_ref, *, local):
    devices, _, _, channels = all_ref.shape
    count = devices * local * (channels // GROUPS)
    out_ref[0] = n_ref[0]
    out_ref[1] = n_ref[3]
    out_ref[2] = jnp.broadcast_to(gain_ref[...], n_ref[0].shape)
    for k in range(2):
        out_ref[3 + k] = over_group(jnp.sum(all_ref[:, k], axis=0) * gain_ref[...]) * (1.0 / count)


def per_image(shape):
    rest = len(shape) - 1
    return pl.BlockSpec((1,) + tuple(shape[1:]), lambda i: (i,) + (0,) * rest)


def whole(shape):
    return pl.BlockSpec(tuple(shape), lambda i: (0,) * len(shape))


SCALARS = pl.BlockSpec(memory_space=pltpu.SMEM)


def call(kernel, images, ins, outs, scratch=(), flops=0):
    nbytes = sum(x.size * x.dtype.itemsize for x, _ in ins)
    shapes = [jax.ShapeDtypeStruct(shape, dtype) for shape, dtype, _ in outs]
    nbytes += sum(s.size * s.dtype.itemsize for s in shapes)
    return pl.pallas_call(
        kernel,
        grid=(images,),
        in_specs=[spec for _, spec in ins],
        out_specs=[spec for _, _, spec in outs],
        out_shape=shapes,
        scratch_shapes=list(scratch),
        compiler_params=kernel_params(),
        cost_estimate=cost(flops, nbytes),
    )(*[x for x, _ in ins])


def img(x):
    return (x, per_image(x.shape))


def all_(x):
    return (x, whole(x.shape))


def small_call(kernel, ins, shape):
    return pl.pallas_call(kernel, out_shape=jax.ShapeDtypeStruct(shape, F32))(*ins)


def weights_kernel(*refs):
    count = len(refs) // 5
    for k in range(count):
        k_ref = refs[k]
        ch = k_ref.shape[2]
        n = 3 * ch
        for turned in (False, True):
            out_ref, low_ref = refs[count + 4 * k + 2 * turned : count + 4 * k + 2 * turned + 2]
            for a in range(3):
                for c in range(3):
                    w = k_ref[2 - a, 2 - c].T if turned else k_ref[a, c]
                    high, low = split(w)
                    out_ref[a * ch : (a + 1) * ch, c * ch : (c + 1) * ch] = high
                    out_ref[a * ch : (a + 1) * ch, n + c * ch : n + (c + 1) * ch] = low
                    if a < 2:
                        low_ref[a * ch : (a + 1) * ch, c * ch : (c + 1) * ch] = high
                    else:
                        out_ref[3 * ch :, c * ch : (c + 1) * ch] = high
            out_ref[3 * ch :, n:] = jnp.zeros((ch, n), BF16)


def prepare(*kernels):
    ch = kernels[0].shape[2]
    shapes = [jax.ShapeDtypeStruct(s, BF16) for s in ((4 * ch, 6 * ch), (2 * ch, 3 * ch))]
    out = pl.pallas_call(
        weights_kernel, out_shape=shapes * (2 * len(kernels)), compiler_params=kernel_params()
    )(*kernels)
    return [out[2 * k : 2 * k + 2] for k in range(2 * len(kernels))]


def after(x, *others):
    return lax.optimization_barrier((x,) + others)[0]


def partner(x, axis, bit):
    return lax.ppermute(x, axis, [(k, k ^ bit) for k in range(lax.axis_size(axis))])


def bits(axis):
    return [1 << k for k in range(lax.axis_size(axis).bit_length() - 1)]


def far_bits():
    low, high = bits("rows")[-2:]
    return low, high, low + high


def gather_sums(x, join):
    for bit in bits("rows")[:-2]:
        x = join(x, partner(x, "rows", bit), bit)
    return jnp.stack([x] + [partner(x, "rows", bit) for bit in far_bits()])


def shift_rows(top_source, bottom_source):
    count = lax.axis_size("rows")
    forward = [(i, i + 1) for i in range(count - 1)]
    backward = [(b, a) for a, b in forward]
    return lax.ppermute(top_source, "rows", forward), lax.ppermute(bottom_source, "rows", backward)


def shift_bands(parts):
    row_devs, count = lax.axis_size("rows"), lax.axis_size("img")
    me = lax.axis_index("img")
    edge = jnp.concatenate([jnp.where(me == 0, p[:, :1], p[:, p.shape[1] - 1 :]) for p in parts], axis=2)
    edge = edge.reshape((count, -1) + edge.shape[1:])
    got = []
    for s in range(count):
        down, up = (count - 1 + s) % count, s
        block = lax.dynamic_index_in_dim(edge, jnp.where(me == 0, up, down), 0, keepdims=False)
        pairs = [(r * count + count - 1, (r + 1) * count + down) for r in range(row_devs - 1)]
        pairs += [(r * count, (r - 1) * count + up) for r in range(1, row_devs)]
        got.append(lax.ppermute(block, ("rows", "img"), pairs))
    got = jnp.stack(got)
    pick = lambda k: lax.dynamic_index_in_dim(got, k, 0, keepdims=False)
    return pick(lax.rem(me + 1, count)), pick(me)


def rotate_img(blocks):
    count = lax.axis_size("img")
    me = lax.axis_index("img")
    pick = lambda k: lax.dynamic_index_in_dim(blocks, lax.rem(k, count), 0, keepdims=False)
    came = [pick(me)]
    for d in range(1, count):
        came.append(lax.ppermute(pick(me + d), "img", [(k, (k + d) % count) for k in range(count)]))
    return came


def img_sources():
    count = lax.axis_size("img")
    me = lax.axis_index("img")
    return [lax.rem(me - d + count, count) for d in range(count)]


def slices(cols, shares):
    units, cuts, seen = cols // 8, [0], 0
    for share in shares[:-1]:
        seen += share
        cuts.append(8 * round(units * seen / sum(shares)))
    cuts.append(cols)
    return [(a, b) for a, b in zip(cuts, cuts[1:]) if b > a]


def swap_rows(x):
    return lax.all_to_all(x, "rows", 0, 0)


def trade(x, axis, bit):
    half = x.shape[0] // 2
    mine = lax.rem(lax.axis_index(axis) // bit, 2)
    keep = lax.dynamic_slice_in_dim(x, mine * half, half, 0)
    give = lax.dynamic_slice_in_dim(x, (1 - mine) * half, half, 0)
    return keep + partner(give, axis, bit)


def untrade(x, axis, bit):
    mine = lax.rem(lax.axis_index(axis) // bit, 2)
    other = partner(x, axis, bit)
    return jnp.where(mine == 0, jnp.concatenate([x, other]), jnp.concatenate([other, x]))


def far_place():
    return lax.axis_index("rows") // far_bits()[0]


def far_trade(x):
    quarter = x.shape[0] // 4
    part = lambda k: lax.dynamic_slice_in_dim(x, k * quarter, quarter, 0)
    place = far_place()
    kept = part(place)
    for d, bit in enumerate(far_bits()):
        kept = kept + partner(part(place ^ (d + 1)), "rows", bit)
    return kept


def far_untrade(x):
    parts = jnp.stack([x] + [partner(x, "rows", bit) for bit in far_bits()])
    place = far_place()
    return jnp.concatenate([lax.dynamic_index_in_dim(parts, place ^ k, 0, keepdims=False) for k in range(4)])


def shards(
    image_in, gain_one, shift_one, kernel_one, bias_one, gain_two, shift_two, kernel_two, bias_two, out_grad
):
    n, rows, cols, ch = image_in.shape
    local = rows * cols
    ext = rows + 2
    wide = cols + MARGIN
    place = lax.axis_index("rows")
    edge = jnp.stack([place > 0, place < lax.axis_size("rows") - 1]).astype(F32)
    edges = (edge, SCALARS)
    row_vec = lambda v: v[None, :]
    conv_flops = 2 * 9 * ch * ch * cols * 3 * n
    pair_shape = (2, n, ch)
    pair = (pair_shape, F32, whole(pair_shape))
    maps = lambda r: ((n, r, cols, ch), F32, per_image((n, r, cols, ch)))
    splits = lambda r: ((n, r, wide, 2 * ch), BF16, per_image((n, r, wide, 2 * ch)))
    taps = ((9, ch, ch), F32, whole((9, ch, ch)))
    row_devs, img_devs = lax.axis_size("rows"), lax.axis_size("img")
    slab = rows // img_devs
    in_cuts = slices(cols, (3, 4, 4))
    out_cuts = slices(cols, (3, 6, 2))
    me = lax.axis_index("img")
    norm = functools.partial(norm_kernel, local=local * row_devs // 4)
    back_norm = functools.partial(back_norm_kernel, local=local * row_devs // 4)
    back_norm_last = functools.partial(back_norm_kernel, local=local * row_devs)
    one_shape = (1, n, ch)
    one = (one_shape, F32, whole(one_shape))

    def join_spread(x, y, bit):
        off = x[0] - y[0]
        return jnp.stack([x[0] + y[0], x[1] + y[1] + off * off * (0.5 / (bit * local))])

    def join_add(x, y, bit):
        return x + y

    grad_in = out_grad.reshape(out_grad.shape[2:])
    landed, came = [], []

    def bring(k, *others):
        a, b = in_cuts[k]
        landed.append(swap_rows(after(grad_in[:, :, a:b], *others)))

    def settle(k, *others):
        a, b = in_cuts[k]
        came.append(rotate_img(after(landed[k], *others).reshape(img_devs, n, slab, b - a, ch)))

    w_one, w_one_back, w_two, w_two_back = prepare(kernel_one, kernel_two)

    top, bottom = shift_rows(image_in[:, rows - 2 :], image_in[:, :2])
    (stat_one,) = call(stats_kernel, n, [img(image_in)], [pair])
    bring(0, stat_one)
    far_one = after(gather_sums(stat_one, join_spread), landed[0], top, bottom)
    n_one = small_call(norm, (far_one, row_vec(gain_one), row_vec(shift_one)), (4, n, ch))
    bring(1, far_one)
    settle(0, far_one)
    middle, act_one, stat_two = call(
        conv_one_kernel,
        n,
        [edges, img(image_in), img(top), img(bottom), all_(n_one), *map(all_, w_one), all_(row_vec(bias_one))],
        [maps(ext), splits(ext), pair],
        [pltpu.VMEM((rows + 4, wide, 2 * ch), BF16)],
        conv_flops * ext,
    )
    far_two = after(gather_sums(after(stat_two, *came[0]), join_spread), landed[1])
    n_two = small_call(norm, (far_two, row_vec(gain_two), row_vec(shift_two)), (4, n, ch))
    bring(2, far_two)
    settle(1, far_two)
    banded_shape = (img_devs, n, slab, cols, ch)
    banded = (banded_shape, F32, pl.BlockSpec((img_devs, 1, slab, cols, ch), lambda i: (0, i, 0, 0, 0)))
    result, act_two = call(
        conv_two_kernel,
        n,
        [edges, img(middle), img(image_in), all_(n_two), *map(all_, w_two), all_(row_vec(bias_two))],
        [banded, splits(ext)],
        (),
        conv_flops * rows,
    )

    def turn(a, b, *others):
        bands = jnp.stack(rotate_img(after(result[..., a:b, :], *others)))
        pick = lambda j: lax.dynamic_index_in_dim(bands, lax.rem(me - j + img_devs, img_devs), 0, keepdims=False)
        return jnp.stack([pick(j) for j in range(img_devs)]).reshape(img_devs * n, slab, b - a, ch)

    mixed_parts = []

    def send(k, *others):
        mixed_parts.append(swap_rows(after(blocks[k], *others)))

    blocks = [turn(*out_cuts[0], *came[1])]
    cut = in_cuts[-1][0]
    offsets = tuple(a for a, _ in in_cuts)
    band = jnp.stack(img_sources()).astype(jnp.int32)

    def add_taps(before, act, parts, at, start, width, bands):
        act_in = img(act)
        if start % width == 0:
            place, start = start // width, 0
            act_in = (act, pl.BlockSpec((1, ext, width, 2 * ch), lambda i: (i, 0, place, 0)))
        return call(
            functools.partial(taps_kernel, offsets=tuple(at), start=start),
            n,
            [all_(before), act_in, (bands, SCALARS)] + [img(p) for line in parts for p in line],
            [taps, one],
            [pltpu.VMEM((rows, width, ch), F32), pltpu.VMEM((rows * width, 6 * ch), BF16)],
            conv_flops * rows * width / wide,
        )

    no_taps = jnp.zeros((9, ch, ch), F32)
    early, late = -(-(cut + 1) // 16) * 16, (cut - 1) // 16 * 16
    by_band = lambda parts: [[part[d] for part in parts] for d in range(img_devs)]
    taps_two, sum_early = add_taps(no_taps, act_two, by_band(came), offsets[:-1], 0, early, band)

    g_top, g_bottom = shift_bands(after(tuple(landed), result))
    settle(2, g_top, g_bottom, blocks[0])
    blocks.append(turn(*out_cuts[1], *came[2]))
    blocks.append(turn(*out_cuts[2], blocks[1]))
    send(0, landed[2], blocks[0], g_top, g_bottom, taps_two)
    grad_result, pre_two, sum_two = call(
        functools.partial(back_two_kernel, offsets=offsets),
        n,
        [(band, SCALARS), img(g_top), img(g_bottom), img(middle), all_(n_two), *map(all_, w_two_back)]
        + [img(p) for line in by_band(came) for p in line],
        [maps(rows), maps(rows), pair],
        [pltpu.VMEM((ext, wide, 2 * ch), BF16)],
        conv_flops * rows,
    )
    pre_top, pre_bottom = shift_rows(pre_two[:, rows - 1 :], pre_two[:, :1])
    far_back = after(gather_sums(sum_two, join_add), mixed_parts[0], blocks[1], pre_top, pre_bottom)
    b_two = small_call(back_norm, (far_back, n_two, row_vec(gain_two)), (5, n, ch))
    send(1, far_back)
    three = ((3, n, ch), F32, whole((3, n, ch)))
    grad_mid, partial, sum_one = call(
        back_one_kernel,
        n,
        [edges, img(pre_two), img(pre_top), img(pre_bottom), img(middle), all_(b_two), img(grad_result), img(image_in), all_(n_one), *map(all_, w_one_back)],
        [maps(rows), maps(rows), three],
        [pltpu.VMEM((ext, wide, 2 * ch), BF16)],
        conv_flops * rows,
    )
    taps_two, sum_late = add_taps(
        taps_two, after(act_two, b_two), by_band(came[-1:]), (cut - late,), late, wide - late, band
    )
    zero = jnp.zeros((1,), jnp.int32)
    taps_one, _ = add_taps(no_taps, after(act_one, blocks[2]), [[grad_mid]], (0,), 0, wide, zero)
    size = 9 * ch
    flat = jnp.concatenate([taps_one.reshape(size, ch), taps_two.reshape(size, ch)])
    steps = [("rows", k) for k in bits("rows")[:-2]] + [("img", k) for k in bits("img")]
    for axis, bit in steps:
        flat = trade(flat, axis, bit)
    sums = jnp.concatenate([sum_one, sum_early + sum_late], axis=0)
    for bit in bits("rows")[:-2]:
        sums = sums + partner(sums, "rows", bit)
    sums_in, flat = after((sums.reshape(-1, ch), flat), mixed_parts[1])
    quarter = flat.shape[0] // 4
    place = lax.axis_index("rows") // far_bits()[0]
    with_sums = lambda k: jnp.concatenate([sums_in, lax.dynamic_slice_in_dim(flat, k * quarter, quarter, 0)])
    both = with_sums(place)
    both = both + sum(partner(with_sums(place ^ (d + 1)), "rows", bit) for d, bit in enumerate(far_bits()))
    far_last, flat = both[: sums_in.shape[0]].reshape((1,) + sums.shape), both[sums_in.shape[0] :]
    flat = jnp.stack([flat] + [partner(flat, "rows", bit) for bit in far_bits()])
    flat = jnp.concatenate([lax.dynamic_index_in_dim(flat, place ^ k, 0, keepdims=False) for k in range(4)])
    b_one = small_call(back_norm_last, (far_last, n_one, row_vec(gain_one)), (5, n, ch))
    empty = jnp.zeros((row_devs, slab, out_cuts[2][1] - out_cuts[2][0], ch), F32)
    mixed = jnp.concatenate(mixed_parts + [empty], axis=2)
    send(2, far_last, flat, mixed)
    (input_grad,) = call(final_kernel, n, [img(partial), img(image_in), all_(b_one)], [maps(rows)])
    for k, (axis, bit) in enumerate(reversed(steps)):
        flat = untrade(flat, axis, bit)
        if k == len(steps) - 1:
            flat = after(flat, input_grad)
    vectors = jnp.concatenate([jnp.sum(far_last, axis=(0, 2)), jnp.sum(far_back, axis=(0, 2))])
    for bit in bits("img"):
        vectors = vectors + partner(vectors, "img", bit)
    last = after(mixed_parts[-1], input_grad, flat, vectors)
    grad_kernel_one, grad_kernel_two = (k.reshape(3, 3, ch, ch) for k in (flat[:size], flat[size:]))
    mixed = lax.dynamic_update_slice_in_dim(mixed, last, out_cuts[2][0], 2)[None, None]
    return (
        mixed,
        input_grad,
        vectors[1],
        vectors[0],
        grad_kernel_one,
        vectors[2],
        vectors[5],
        vectors[4],
        grad_kernel_two,
        vectors[3],
    )


def solution(mesh):
    spread = P("img", "rows", None, None)
    banded = P("rows", "img", None, None, None, None)
    return jax.shard_map(
        shards,
        mesh=mesh,
        in_specs=(spread,) + (P(),) * 8 + (banded,),
        out_specs=(banded, spread) + (P(),) * 8,
        check_vma=False,
    )
```
